128 devices in a mesh: seq: 32 (over x, z, y_lo), head: 4 (over y_hi, core).
Axes of the slice: x: 4, y: 4 (y_hi: 2, y_lo: 2; y = y_hi * 2 + y_lo), z: 4, core: 2. Of those that a mesh axis runs over, the one named last changes fastest.
Arguments:
- tokens_in: bfloat16 [1024, 32, 6144], P('seq', None, 'head'), may hold values from -6 to 6
- gate_rows: bfloat16 [1024, 32, 6144], P('seq', None, 'head'), may hold values from -28 to 28
- gate_cols: bfloat16 [1024, 32, 6144], P(None, 'seq', 'head'), may hold values from -28 to 28
- write_rows: bfloat16 [64, 32768], P(None, 'seq'), may hold values from -6 to 6
- read_rows: bfloat16 [64, 32768], P(None, 'seq'), may hold values from -0.75 to 0.75
- step_rows: float32 [48, 32768], P('head', 'seq'), may hold values from 0 to 2, as said below
- decay_rows: float32 [48, 32768], P('head', 'seq'), may hold values from -1 to 0, as said below
- skip_rows: float32 [48], P('head'), may hold values from 0.5 to 2
- norm_rows: float32 [6144], P('head'), may hold values from 0.5 to 1.5
- write_cols: bfloat16 [64, 32768], P(None, 'seq'), may hold values from -6 to 6
- read_cols: bfloat16 [64, 32768], P(None, 'seq'), may hold values from -0.75 to 0.75
- step_cols: float32 [48, 32768], P('head', 'seq'), may hold values from 0 to 2, as said below
- decay_cols: float32 [48, 32768], P('head', 'seq'), may hold values from -1 to 0, as said below
- skip_cols: float32 [48], P('head'), may hold values from 0.5 to 2
- norm_cols: float32 [6144], P('head'), may hold values from 0.5 to 1.5
Outputs:
- mixed_cols: bfloat16 [1024, 32, 6144], P(None, 'seq', 'head')
The draws below stay inside these ranges and needn't reach their ends.
Inputs may be any that keep to these rules, and one draw needn't show every extreme that they name: `step_rows`: positive. `step_cols`: positive. `decay_rows`: never positive. `decay_cols`: never positive.
All inputs are finite; a program needn't handle non-finite values.
Results may differ from the reference program's by a relative error of at most 0.0063.
Values may be sent and summed in bfloat16 or wider, within the bound.
No kernel may reach another device: no remote copies, remote signals or barrier semaphores. Data moves between devices by JAX's collectives and lax.ppermute only.
A program may use at most 128 MiB of HBM per device.

```python
import math
import jax
import jax.numpy as jnp
from jax import lax

HEADS = 48
HEADDIM = 128
NSTATE = 64
BLOCK = 256
GRID_W = 32
ROWS = 1024
LENGTH = 32768
INNER = 6144


def head_laws(key, salt):
    folded = jax.random.fold_in(key, salt)
    keys = jax.random.split(folded, 7)
    share = 0.5
    slow_heads = jax.random.uniform(keys[0], (HEADS,)) < share
    slow_rate = jax.random.uniform(keys[1], (HEADS,), minval=0.05, maxval=0.5) / LENGTH
    fast_rate = jax.random.uniform(keys[2], (HEADS,), minval=1.0 / 50.0, maxval=1.0 / 30.0)
    each_head_values = jnp.where(slow_heads, slow_rate, fast_rate)
    coarse_estimate = jax.random.uniform(keys[3], (HEADS, LENGTH), minval=0.5, maxval=1.5)
    spread = jax.random.uniform(keys[6], (HEADS, LENGTH), minval=0.5, maxval=1.5)
    grid_points = jax.random.randint(keys[4], (2,), 0, LENGTH)
    retained_values = jax.random.uniform(keys[5], (2,), minval=0.5, maxval=0.8)
    token_locations = jnp.arange(LENGTH, dtype=jnp.int32)
    sudden_jump = jnp.sum(jnp.where(token_locations[None, :] == grid_points[:, None], jnp.log(retained_values)[:, None], 0.0), axis=0)
    decay_factors = -each_head_values[:, None] * coarse_estimate + sudden_jump[None, :]
    scales = jnp.where(slow_heads, jnp.sqrt(40.0 / LENGTH), 1.0)
    steps = scales[:, None] * spread
    return (steps.astype(jnp.float32), decay_factors.astype(jnp.float32))


def gate_draw(key, salt):
    folded = jax.random.fold_in(key, salt)
    head_index = jnp.arange(INNER, dtype=jnp.int32) // HEADDIM
    fraction = head_index.astype(jnp.float32) / (HEADS - 1)
    scales = 4.0 ** fraction
    values = jnp.clip(jax.random.normal(folded, (ROWS, GRID_W, INNER)), -3.0, 3.0)
    return (values * scales).astype(jnp.bfloat16)


def draw_gate_rows(key, part):
    return gate_draw(key, 31)


def draw_gate_cols(key, part):
    return gate_draw(key, 37)


def draw_step_rows(key, part):
    return head_laws(key, 11)[0]


def draw_decay_rows(key, part):
    return head_laws(key, 11)[1]


def draw_step_cols(key, part):
    return head_laws(key, 23)[0]


def draw_decay_cols(key, part):
    return head_laws(key, 23)[1]


def steps_of(own_key, dims, cuts, smallest, high):
    gain = 1.0
    for axis_at, blocks in cuts:
        draws = jax.random.uniform(jax.random.fold_in(jax.random.fold_in(own_key, 6), axis_at), (blocks,), jnp.float32, smallest / len(cuts), high / len(cuts))
        gain = gain * jnp.repeat(jnp.exp(draws), dims[axis_at] // blocks).reshape((-1,) + (1,) * (len(dims) - 1 - axis_at))
    return gain


def centred(rng, extent, scale, limit, cuts=(), kind=jnp.bfloat16):
    array = jax.random.normal(rng, extent, jnp.float32) * scale
    if len(cuts) > 0:
        array = steps_of(rng, extent, cuts, -0.22, 0.18) * array
    return jnp.clip(array, min=-limit, max=limit).astype(kind)


def setup_inputs(seed: int = 0) -> dict:
    arg_keys = jax.random.split(jax.random.key(seed), 16)
    tokens_in = centred(arg_keys[0], (ROWS, GRID_W, INNER), 1.0, 6.0, ((0, 32), (2, 4)))
    gate_rows = draw_gate_rows(jax.random.fold_in(arg_keys[15], 71), 0)
    gate_cols = draw_gate_cols(jax.random.fold_in(arg_keys[15], 71), 0)
    write_rows = centred(arg_keys[3], (NSTATE, LENGTH), 1.0, 6.0, ((1, 32),))
    read_rows = centred(arg_keys[4], (NSTATE, LENGTH), NSTATE ** -0.5, 0.75, ((1, 32),))
    step_rows = draw_step_rows(jax.random.fold_in(arg_keys[15], 71), 0)
    decay_rows = draw_decay_rows(jax.random.fold_in(arg_keys[15], 71), 0)
    skip_rows = jnp.clip(jnp.exp(math.log(2.0) - 1.3862944 * jax.random.uniform(arg_keys[7], (HEADS,), jnp.float32) ** steps_of(arg_keys[7], (HEADS,), ((0, 4),), -0.2, 0.2)), 0.5, 2.0)
    norm_rows = jnp.clip(1.0 + 0.1 * jax.random.normal(arg_keys[8], (INNER,), jnp.float32), 0.5, 1.5)
    write_cols = centred(arg_keys[9], (NSTATE, LENGTH), 1.0, 6.0, ((1, 32),))
    read_cols = centred(arg_keys[10], (NSTATE, LENGTH), NSTATE ** -0.5, 0.75, ((1, 32),))
    step_cols = draw_step_cols(jax.random.fold_in(arg_keys[15], 71), 0)
    decay_cols = draw_decay_cols(jax.random.fold_in(arg_keys[15], 71), 0)
    skip_cols = jnp.clip(jnp.exp(math.log(2.0) - 1.3862944 * jax.random.uniform(arg_keys[13], (HEADS,), jnp.float32) ** steps_of(arg_keys[13], (HEADS,), ((0, 4),), -0.2, 0.2)), 0.5, 2.0)
    norm_cols = jnp.clip(1.0 + 0.1 * jax.random.normal(arg_keys[14], (INNER,), jnp.float32), 0.5, 1.5)
    return dict(tokens_in=tokens_in, gate_rows=gate_rows, gate_cols=gate_cols, write_rows=write_rows, read_rows=read_rows, step_rows=step_rows, decay_rows=decay_rows, skip_rows=skip_rows, norm_rows=norm_rows, write_cols=write_cols, read_cols=read_cols, step_cols=step_cols, decay_cols=decay_cols, skip_cols=skip_cols, norm_cols=norm_cols)


EPSILON = 1e-05
HIGHEST = lax.Precision.HIGHEST

def block_step(state_in, inputs, gate_blk, write_blk, read_blk, step_blk, decay_blk, skip_vec, gain_vec):
    length = inputs.shape[0]
    causal = lax.broadcasted_iota(jnp.int32, (length, length), 0) >= lax.broadcasted_iota(jnp.int32, (length, length), 1)
    cumulative = jnp.cumsum(decay_blk, axis=1)
    scores = jnp.dot(read_blk.T, write_blk, preferred_element_type=jnp.float32)
    spread = cumulative[:, :, None] - cumulative[:, None, :]
    fading = jnp.where(causal, jnp.exp(jnp.where(causal, spread, 0.0)), 0.0)
    mixing = (fading * scores[None] * step_blk[:, None, :]).astype(jnp.bfloat16)
    wide_in = inputs.astype(jnp.float32)
    inner_part = jnp.einsum('hts,shp->thp', mixing.astype(jnp.float32), wide_in)
    tail_weights = jnp.exp(cumulative[:, -1:] - cumulative) * step_blk
    loaded = (write_blk.astype(jnp.float32)[None] * tail_weights[:, None, :]).astype(jnp.bfloat16)
    gained = jnp.einsum('hns,shp->hnp', loaded.astype(jnp.float32), wide_in)
    from_state = jnp.einsum('nt,hnp->thp', read_blk.astype(jnp.float32), state_in, precision=HIGHEST)
    outputs = inner_part + from_state * jnp.exp(cumulative).T[:, :, None] + skip_vec[:, None] * wide_in
    gated = outputs.reshape(length, -1) * jax.nn.silu(gate_blk.astype(jnp.float32))
    scaled = lax.rsqrt(lax.optimization_barrier(jnp.mean(gated * gated, axis=-1)) + EPSILON)
    result = (gated * scaled[:, None] * gain_vec).astype(jnp.bfloat16)
    new_state = jnp.exp(cumulative[:, -1])[:, None, None] * state_in + gained
    return (new_state, result)

def run_layer(fetch, block_total, write_mat, read_mat, step_mat, decay_mat, skip_vec, gain_vec):
    head_count = step_mat.shape[0]
    state_size = write_mat.shape[0]
    head_width = gain_vec.shape[0] // head_count

    def window_of(matrix, offset):
        return lax.dynamic_slice_in_dim(matrix, offset, BLOCK, 1)

    def advance(state_in, block_index):
        inputs, gate_blk = fetch(block_index)
        offset = (block_index * BLOCK).astype(jnp.int32)
        return block_step(state_in, inputs, gate_blk, window_of(write_mat, offset), window_of(read_mat, offset), window_of(step_mat, offset), window_of(decay_mat, offset), skip_vec, gain_vec)
    initial = jnp.zeros((head_count, state_size, head_width), jnp.float32)
    return lax.scan(advance, initial, jnp.arange(block_total, dtype=jnp.int32))[1]

def reference(tokens_in, gate_rows, gate_cols, write_rows, read_rows, step_rows, decay_rows, skip_rows, norm_rows, write_cols, read_cols, step_cols, decay_cols, skip_cols, norm_cols):
    flat_tokens = tokens_in.reshape(LENGTH, INNER)
    flat_gate = gate_rows.reshape(LENGTH, INNER)

    def fetch_rows(block_index):
        offset = (block_index * BLOCK).astype(jnp.int32)
        token_block = lax.dynamic_slice_in_dim(flat_tokens, offset, BLOCK, 0).reshape(BLOCK, HEADS, HEADDIM)
        return (token_block, lax.dynamic_slice_in_dim(flat_gate, offset, BLOCK, 0))
    first = run_layer(fetch_rows, LENGTH // BLOCK, write_rows, read_rows, step_rows, decay_rows, skip_rows, norm_rows)
    hidden = first.reshape(ROWS, GRID_W, INNER)
    per_col = ROWS // BLOCK

    def fetch_cols(block_index):
        column = (block_index // per_col).astype(jnp.int32)
        row_start = (block_index % per_col * BLOCK).astype(jnp.int32)
        zero_index = jnp.zeros((), jnp.int32)
        token_block = lax.dynamic_slice(hidden, (row_start, column, zero_index), (BLOCK, 1, INNER)).reshape(BLOCK, HEADS, HEADDIM)
        gate_block = lax.dynamic_slice(gate_cols, (row_start, column, zero_index), (BLOCK, 1, INNER)).reshape(BLOCK, INNER)
        return (token_block, gate_block)
    second = run_layer(fetch_cols, LENGTH // BLOCK, write_cols, read_cols, step_cols, decay_cols, skip_cols, norm_cols)
    return second.reshape(GRID_W, per_col, BLOCK, INNER).transpose(1, 2, 0, 3).reshape(ROWS, GRID_W, INNER)
```

```python
import functools

import jax
import jax.numpy as jnp
from jax import lax
from jax.experimental import pallas as pl
from jax.experimental.pallas import tpu as pltpu
from jax.sharding import Mesh
from jax.sharding import PartitionSpec as P

BLOCK = 256
SEQ = ("seq_0", "seq_1", "seq_2")
EPSILON = 1e-05
LANES = 128
TILE = 8
HEADS_PER_STEP = 3
VMEM_LIMIT = 40 * 1024 * 1024
F32 = jnp.float32
BF16 = jnp.bfloat16


def params():
    return pltpu.CompilerParams(vmem_limit_bytes=VMEM_LIMIT)


def split_three(value):
    high = value.astype(BF16)
    rest = value - high.astype(F32)
    middle = rest.astype(BF16)
    low = (rest - middle.astype(F32)).astype(BF16)
    return high, middle, low


def running_sums(decay):
    length = decay.shape[1]
    earlier = lax.broadcasted_iota(jnp.int32, (length, length), 0)
    later = lax.broadcasted_iota(jnp.int32, (length, length), 1)
    upper = jnp.where(earlier <= later, 1.0, 0.0).astype(BF16)
    high, middle, low = split_three(decay)
    total = jnp.dot(low, upper, preferred_element_type=F32)
    total = total + jnp.dot(middle, upper, preferred_element_type=F32)
    return total + jnp.dot(high, upper, preferred_element_type=F32)


def norm_scale(squares, features):
    return lax.rsqrt(squares / features + EPSILON)


def head_inputs(x_ref, head, by_head):
    if by_head:
        rows = x_ref.shape[1] // 12
        return x_ref[:, head * rows : (head + 1) * rows, :].reshape(BLOCK, LANES)
    return x_ref[:, head * LANES : (head + 1) * LANES]


def states_kernel(by_head, features, *refs):
    if by_head:
        x_ref, write_ref, step_ref, decay_ref, squares_ref, payload_ref, before_ref, state, total = refs
    else:
        x_ref, write_ref, step_ref, decay_ref, payload_ref, before_ref, state, total = refs
    head_count = step_ref.shape[0]
    state_size = write_ref.shape[0]
    block = pl.program_id(0)

    @pl.when(block == 0)
    def _():
        state[...] = jnp.zeros_like(state)
        total[...] = jnp.zeros_like(total)

    before_ref[0] = state[...]
    cumulative = running_sums(decay_ref[...])
    final = cumulative[:, BLOCK - 1 :]
    weights = jnp.exp(final - cumulative) * step_ref[...]
    if by_head:
        weights = weights * norm_scale(squares_ref[...], features)
    fading = jnp.broadcast_to(jnp.exp(final), (head_count, LANES))
    write = write_ref[...].astype(F32)
    for head in range(head_count):
        loaded = (write * weights[head : head + 1, :]).astype(BF16)
        gained = jnp.dot(loaded, head_inputs(x_ref, head, by_head), preferred_element_type=F32)
        rows = slice(head * state_size, (head + 1) * state_size)
        state[rows, :] = fading[head : head + 1, :] * state[rows, :] + gained
    total[...] = total[...] + jnp.broadcast_to(final, (head_count, LANES))

    @pl.when(block == pl.num_programs(0) - 1)
    def _():
        devices, height = payload_ref.shape[0], payload_ref.shape[1] - TILE
        payload_ref[:, :height, :] = state[...].reshape(devices, height, LANES)
        for device in range(devices):
            for tile in range(height // TILE):
                head = (device * height + tile * TILE) // state_size
                payload_ref[device, height + tile : height + tile + 1, :] = total[head : head + 1, :]
            left = height + height // TILE
            payload_ref[device, left:, :] = jnp.zeros((height + TILE - left, LANES), F32)


def device_states(x, write, step, decay, squares, features, devices):
    head_count, length = step.shape
    state_size = write.shape[0]
    blocks = length // BLOCK
    height = head_count * state_size // devices
    by_head = squares is not None
    if by_head:
        x_spec = pl.BlockSpec((x.shape[0] // blocks, *x.shape[1:]), lambda k: (k, 0, 0))
    else:
        x_spec = pl.BlockSpec((BLOCK, x.shape[1]), lambda k: (k, 0))
    along = lambda rows: pl.BlockSpec((rows, BLOCK), lambda k: (0, k))
    specs = [x_spec, along(state_size), along(head_count), along(head_count)]
    operands = [x, write, step, decay]
    if by_head:
        specs.append(along(1))
        operands.append(squares)
    return pl.pallas_call(
        functools.partial(states_kernel, by_head, features),
        grid=(blocks,),
        in_specs=specs,
        out_specs=[
            pl.BlockSpec((devices, height + TILE, LANES), lambda k: (0, 0, 0)),
            pl.BlockSpec((1, head_count * state_size, LANES), lambda k: (k, 0, 0)),
        ],
        out_shape=[
            jax.ShapeDtypeStruct((devices, height + TILE, LANES), F32),
            jax.ShapeDtypeStruct((blocks, head_count * state_size, LANES), F32),
        ],
        scratch_shapes=[
            pltpu.VMEM((head_count * state_size, LANES), F32),
            pltpu.VMEM((head_count, LANES), F32),
        ],
        compiler_params=params(),
        cost_estimate=pl.CostEstimate(flops=500_000_000, bytes_accessed=6_000_000, transcendentals=20_000),
        name="states",
    )(*operands)


def prefix_kernel(ends_ref, prior_ref):
    devices, height, _ = prior_ref.shape
    running = [jnp.zeros((TILE, LANES), F32) for _ in range(height // TILE)]
    for device in range(devices):
        for tile in range(height // TILE):
            rows = slice(tile * TILE, (tile + 1) * TILE)
            prior_ref[device, rows, :] = running[tile]
            fade = jnp.exp(ends_ref[device, height + tile : height + tile + 1, :])
            running[tile] = fade * running[tile] + ends_ref[device, rows, :]


def prior_states(payload):
    devices, height, _ = payload.shape
    height = height - TILE
    ends = lax.all_to_all(payload, SEQ, split_axis=0, concat_axis=0, tiled=True)
    prior = pl.pallas_call(
        prefix_kernel,
        out_shape=jax.ShapeDtypeStruct((devices, height, LANES), F32),
        compiler_params=params(),
        name="prefix",
    )(ends)
    prior = lax.all_to_all(prior, SEQ, split_axis=0, concat_axis=0, tiled=True)
    return prior.reshape(devices * height, LANES)


def read_state(read, state):
    parts = jnp.concatenate(split_three(state), axis=0)
    wide = jnp.concatenate([read, read, read], axis=0)
    return lax.dot_general(wide, parts, (((0,), (0,)), ((), ())), preferred_element_type=F32)


def local_kernel(by_head, features, *refs):
    if by_head:
        x_ref, write_ref, read_ref, step_ref, decay_ref, squares_ref, before_ref, skip_ref, out_ref, lift_ref, total = refs
    else:
        x_ref, write_ref, read_ref, step_ref, decay_ref, before_ref, skip_ref, out_ref, lift_ref, total = refs
    head_count = step_ref.shape[0]
    state_size = write_ref.shape[0]
    block = pl.program_id(0)
    half = BLOCK // 2

    @pl.when(block == 0)
    def _():
        total[...] = jnp.zeros_like(total)

    cumulative = running_sums(decay_ref[...])
    step = step_ref[...]
    if by_head:
        scale = norm_scale(squares_ref[...], features)
        step = step * scale
        scale_column = jnp.transpose(jnp.broadcast_to(scale, (LANES, BLOCK)))
    padding = jnp.zeros((LANES - head_count, BLOCK), F32)
    columns = jnp.transpose(jnp.concatenate([cumulative, padding], axis=0))
    whole = jnp.concatenate([cumulative + total[:, :1], padding], axis=0)
    lift_ref[...] = jnp.exp(jnp.transpose(whole))
    total[...] = total[...] + jnp.broadcast_to(cumulative[:, BLOCK - 1 :], (head_count, LANES))
    read = read_ref[...]
    scores = lax.dot_general(read, write_ref[...], (((0,), (0,)), ((), ())), preferred_element_type=F32)
    first, last = slice(0, half), slice(half, BLOCK)
    causal = lax.broadcasted_iota(jnp.int32, (half, half), 0) >= lax.broadcasted_iota(
        jnp.int32, (half, half), 1
    )
    for head in range(head_count):
        row = cumulative[head : head + 1, :]
        column = jnp.broadcast_to(columns[:, head : head + 1], (BLOCK, LANES))
        weight = step[head : head + 1, :]

        def mixing(t, s):
            spread = column[t] - row[:, s]
            if t == s:
                spread = jnp.where(causal, spread, -jnp.inf)
            return (jnp.exp(spread) * scores[t, s] * weight[:, s]).astype(BF16)

        x = head_inputs(x_ref, head, by_head)
        upper = jnp.dot(mixing(first, first), x[first], preferred_element_type=F32)
        both = jnp.concatenate([mixing(last, first), mixing(last, last)], axis=1)
        lower = jnp.dot(both, x, preferred_element_type=F32)
        state = before_ref[0, head * state_size : (head + 1) * state_size, :]
        outputs = jnp.concatenate([upper, lower], axis=0) + jnp.exp(column) * read_state(read, state)
        skipped = skip_ref[head] * x.astype(F32)
        if by_head:
            skipped = skipped * scale_column
        out_ref[:, head * LANES : (head + 1) * LANES] = outputs + skipped


def local_outputs(x, write, read, step, decay, squares, before, skip, features):
    head_count, length = step.shape
    state_size = write.shape[0]
    blocks = length // BLOCK
    by_head = squares is not None
    if by_head:
        x_spec = pl.BlockSpec((x.shape[0] // blocks, *x.shape[1:]), lambda k: (k, 0, 0))
    else:
        x_spec = pl.BlockSpec((BLOCK, x.shape[1]), lambda k: (k, 0))
    along = lambda rows: pl.BlockSpec((rows, BLOCK), lambda k: (0, k))
    specs = [x_spec, along(state_size), along(state_size), along(head_count), along(head_count)]
    operands = [x, write, read, step, decay]
    if by_head:
        specs.append(along(1))
        operands.append(squares)
    specs.append(pl.BlockSpec((1, head_count * state_size, LANES), lambda k: (k, 0, 0)))
    specs.append(pl.BlockSpec(memory_space=pltpu.SMEM))
    operands += [before, skip]
    width = head_count * LANES
    return pl.pallas_call(
        functools.partial(local_kernel, by_head, features),
        grid=(blocks,),
        in_specs=specs,
        out_specs=[
            pl.BlockSpec((BLOCK, width), lambda k: (k, 0)),
            pl.BlockSpec((BLOCK, LANES), lambda k: (k, 0)),
        ],
        out_shape=[
            jax.ShapeDtypeStruct((length, width), F32),
            jax.ShapeDtypeStruct((length, LANES), F32),
        ],
        scratch_shapes=[pltpu.VMEM((head_count, LANES), F32)],
        compiler_params=params(),
        cost_estimate=pl.CostEstimate(
            flops=6_000_000_000, bytes_accessed=12_000_000, transcendentals=3_000_000
        ),
        name="local",
    )(*operands)


def gated_kernel(first_layer, local_ref, lift_ref, read_ref, prior_ref, gate_ref, gain_ref, *refs):
    if first_layer:
        out_ref, squares_ref, total, staged = refs
    else:
        out_ref, squares_ref, total = refs
    group = pl.program_id(0)
    length = local_ref.shape[0]
    heads = local_ref.shape[1] // LANES
    state_size = read_ref.shape[0]
    cols = out_ref.shape[0]
    rows = length // cols

    @pl.when(group == 0)
    def _():
        total[...] = jnp.zeros_like(total)

    read = read_ref[...]
    chosen = lax.broadcasted_iota(jnp.int32, (length, LANES), 1)
    for head in range(heads):
        place = slice(head * LANES, (head + 1) * LANES)
        state = prior_ref[head * state_size : (head + 1) * state_size, :]
        at = group * heads + head
        lift = jnp.sum(jnp.where(chosen == at, lift_ref[...], 0.0), axis=1, keepdims=True)
        outputs = local_ref[:, place] + lift * read_state(read, state)
        gate = gate_ref[:, place].astype(F32)
        gated = outputs * (gate / (1.0 + jnp.exp(-gate)))
        total[...] += gated * gated
        gated = gated * gain_ref[:, place]
        if first_layer:
            staged[...] = gated
            for col in range(cols):
                picked = staged[pl.ds(col, rows, stride=cols), :]
                out_ref[col, head * rows : (head + 1) * rows, :] = picked.astype(BF16)
        else:
            out_ref[:, place] = gated

    @pl.when(group == pl.num_programs(0) - 1)
    def _():
        if first_layer:
            ordered = jnp.concatenate(
                [total[pl.ds(col, rows, stride=cols), :] for col in range(cols)], axis=0
            )
        else:
            ordered = total[...]
        ones = jnp.ones((TILE, LANES), BF16)
        sums = jnp.zeros((TILE, length), F32)
        for part in split_three(ordered):
            sums = sums + lax.dot_general(
                ones, part, (((1,), (1,)), ((), ())), preferred_element_type=F32
            )
        squares_ref[...] = sums[:1]


def gated_outputs(first_layer, local, lift, read, prior, gate, gain, cols):
    length, width = local.shape
    state_size = read.shape[0]
    heads = HEADS_PER_STEP
    part = heads * LANES
    groups = width // part
    if first_layer:
        rows = length // cols
        out_spec = pl.BlockSpec((cols, heads * rows, LANES), lambda g: (0, g, 0))
        out_shape = jax.ShapeDtypeStruct((cols, width // LANES * rows, LANES), BF16)
        scratch = [pltpu.VMEM((length, LANES), F32), pltpu.VMEM((length, LANES), F32)]
    else:
        out_spec = pl.BlockSpec((length, part), lambda g: (0, g))
        out_shape = jax.ShapeDtypeStruct((length, width), F32)
        scratch = [pltpu.VMEM((length, LANES), F32)]
    return pl.pallas_call(
        functools.partial(gated_kernel, first_layer),
        grid=(groups,),
        in_specs=[
            pl.BlockSpec((length, part), lambda g: (0, g)),
            pl.BlockSpec((length, LANES), lambda g: (0, 0)),
            pl.BlockSpec((state_size, length), lambda g: (0, 0)),
            pl.BlockSpec((heads * state_size, LANES), lambda g: (g, 0)),
            pl.BlockSpec((length, part), lambda g: (0, g)),
            pl.BlockSpec((1, part), lambda g: (0, g)),
        ],
        out_specs=[out_spec, pl.BlockSpec((1, length), lambda g: (0, 0))],
        out_shape=[out_shape, jax.ShapeDtypeStruct((1, length), F32)],
        scratch_shapes=scratch,
        compiler_params=params(),
        cost_estimate=pl.CostEstimate(
            flops=1_200_000_000, bytes_accessed=13_000_000, transcendentals=2_000_000
        ),
        name="gated",
    )(local, lift, read, prior, gate, gain)


def scaled_kernel(features, gated_ref, squares_ref, out_ref):
    scale = norm_scale(squares_ref[...], features)
    column = jnp.transpose(jnp.broadcast_to(scale, (LANES, scale.shape[1])))
    for head in range(gated_ref.shape[1] // LANES):
        place = slice(head * LANES, (head + 1) * LANES)
        out_ref[:, place] = (gated_ref[:, place] * column).astype(BF16)


def scaled_outputs(gated, squares, features):
    length, width = gated.shape
    return pl.pallas_call(
        functools.partial(scaled_kernel, features),
        grid=(length // BLOCK,),
        in_specs=[
            pl.BlockSpec((BLOCK, width), lambda k: (k, 0)),
            pl.BlockSpec((1, BLOCK), lambda k: (0, k)),
        ],
        out_specs=pl.BlockSpec((BLOCK, width), lambda k: (k, 0)),
        out_shape=jax.ShapeDtypeStruct((length, width), BF16),
        compiler_params=params(),
        name="scaled",
    )(gated, squares)


def column_squares(squares, devices):
    whole = lax.psum(squares, "head")[0]
    for axis in reversed(SEQ):
        whole = lax.all_gather(whole, axis)
    whole = whole.reshape(devices, devices, -1)
    mine = lax.dynamic_index_in_dim(whole, lax.axis_index(SEQ), axis=1, keepdims=False)
    return mine.reshape(1, -1)


def body(
    tokens_in,
    gate_rows,
    gate_cols,
    write_rows,
    read_rows,
    step_rows,
    decay_rows,
    skip_rows,
    norm_rows,
    write_cols,
    read_cols,
    step_cols,
    decay_cols,
    skip_cols,
    norm_cols,
):
    grid_rows, grid_cols, width = tokens_in.shape
    devices = lax.axis_size(SEQ)
    features = float(width * lax.axis_size("head"))
    tokens = grid_rows * grid_cols
    column_len = gate_cols.shape[0]

    x = tokens_in.reshape(tokens, width)
    payload, before = device_states(x, write_rows, step_rows, decay_rows, None, features, devices)
    prior = prior_states(payload)
    local, lift = local_outputs(
        x, write_rows, read_rows, step_rows, decay_rows, None, before, skip_rows, features
    )
    hidden, squares = gated_outputs(
        True, local, lift, read_rows, prior, gate_rows.reshape(tokens, width), norm_rows[None], grid_cols
    )
    hidden = lax.all_to_all(hidden, SEQ, split_axis=0, concat_axis=0, tiled=True)
    squares = column_squares(squares, devices)

    payload, before = device_states(
        hidden, write_cols, step_cols, decay_cols, squares, features, devices
    )
    prior = prior_states(payload)
    local, lift = local_outputs(
        hidden, write_cols, read_cols, step_cols, decay_cols, squares, before, skip_cols, features
    )
    gated, squares = gated_outputs(
        False, local, lift, read_cols, prior, gate_cols.reshape(column_len, width), norm_cols[None], 1
    )
    squares = lax.psum(squares, "head")
    out = scaled_outputs(gated, squares, features)
    return out.reshape(column_len, 1, width)


def solution(mesh):
    torus = Mesh(
        mesh.devices.reshape(4, 4, 2, mesh.shape["head"]), ("seq_0", "seq_1", "seq_2", "head")
    )
    return jax.shard_map(
        body,
        mesh=torus,
        in_specs=(
            P(SEQ, None, "head"),
            P(SEQ, None, "head"),
            P(None, SEQ, "head"),
            P(None, SEQ),
            P(None, SEQ),
            P("head", SEQ),
            P("head", SEQ),
            P("head"),
            P("head"),
            P(None, SEQ),
            P(None, SEQ),
            P("head", SEQ),
            P("head", SEQ),
            P("head"),
            P("head"),
        ),
        out_specs=P(None, SEQ, "head"),
        check_vma=False,
    )
```

```python
import functools

import jax
import jax.numpy as jnp
from jax import lax
from jax.experimental import pallas as pl
from jax.experimental.pallas import tpu as pltpu
from jax.sharding import Mesh
from jax.sharding import PartitionSpec as P

BLOCK = 256
SEQ = ("seq_0", "seq_1", "seq_2")
EPSILON = 1e-05
LANES = 128
TILE = 8
HEADS_PER_STEP = 2
EXTRA = 16
MEGABYTE = 1024 * 1024
F32 = jnp.float32
BF16 = jnp.bfloat16


def params(megabytes=56):
    return pltpu.CompilerParams(vmem_limit_bytes=megabytes * MEGABYTE)


def split_three(value):
    high = value.astype(BF16)
    rest = value - high.astype(F32)
    middle = rest.astype(BF16)
    low = (rest - middle.astype(F32)).astype(BF16)
    return high, middle, low


def running_sums(decay):
    length = decay.shape[1]
    earlier = lax.broadcasted_iota(jnp.int32, (length, length), 0)
    later = lax.broadcasted_iota(jnp.int32, (length, length), 1)
    upper = jnp.where(earlier <= later, 1.0, 0.0).astype(BF16)
    high, middle, low = split_three(decay)
    total = jnp.dot(low, upper, preferred_element_type=F32)
    total = total + jnp.dot(middle, upper, preferred_element_type=F32)
    return total + jnp.dot(high, upper, preferred_element_type=F32)


def norm_scale(squares, features):
    return lax.rsqrt(squares / features + EPSILON)


def head_inputs(x_ref, head, by_head):
    if by_head:
        rows = BLOCK // x_ref.shape[0]
        return x_ref[:, head * rows : (head + 1) * rows, :].reshape(BLOCK, LANES)
    return x_ref[:, head * LANES : (head + 1) * LANES]


def block_scale(squares_ref, features):
    pieces = [squares_ref[device : device + 1, :] for device in range(squares_ref.shape[0])]
    return norm_scale(jnp.concatenate(pieces, axis=1), features)


def states_kernel(by_head, features, *refs):
    if by_head:
        x_ref, write_ref, step_ref, decay_ref, squares_ref, payload_ref, before_ref, state, total = refs
    else:
        x_ref, write_ref, step_ref, decay_ref, payload_ref, before_ref, state, total = refs
    head_count = step_ref.shape[0]
    state_size = write_ref.shape[0]
    block = pl.program_id(0)

    @pl.when(block == 0)
    def _():
        state[...] = jnp.zeros_like(state)
        total[...] = jnp.zeros_like(total)

    before_ref[0] = state[...]
    cumulative = running_sums(decay_ref[...])
    final = cumulative[:, BLOCK - 1 :]
    weights = jnp.exp(final - cumulative) * step_ref[...]
    if by_head:
        weights = weights * block_scale(squares_ref, features)
    fading = jnp.broadcast_to(jnp.exp(final), (head_count, LANES))
    write = write_ref[...].astype(F32)
    for head in range(head_count):
        loaded = (write * weights[head : head + 1, :]).astype(BF16)
        gained = jnp.dot(loaded, head_inputs(x_ref, head, by_head), preferred_element_type=F32)
        rows = slice(head * state_size, (head + 1) * state_size)
        state[rows, :] = fading[head : head + 1, :] * state[rows, :] + gained
    total[...] = total[...] + jnp.broadcast_to(final, (head_count, LANES))

    @pl.when(block == pl.num_programs(0) - 1)
    def _():
        devices, height = payload_ref.shape[0], payload_ref.shape[1] - TILE
        payload_ref[:, :height, :] = state[...].reshape(devices, height, LANES)
        for device in range(devices):
            for tile in range(height // TILE):
                head = (device * height + tile * TILE) // state_size
                payload_ref[device, height + tile : height + tile + 1, :] = total[head : head + 1, :]
            left = height + height // TILE
            payload_ref[device, left:, :] = jnp.zeros((height + TILE - left, LANES), F32)


def device_states(x, write, step, decay, squares, features, devices):
    head_count, length = step.shape
    state_size = write.shape[0]
    blocks = length // BLOCK
    height = head_count * state_size // devices
    by_head = squares is not None
    if by_head:
        x_spec = pl.BlockSpec((x.shape[0] // blocks, *x.shape[1:]), lambda k: (k, 0, 0))
    else:
        x_spec = pl.BlockSpec((BLOCK, x.shape[1]), lambda k: (k, 0))
    along = lambda rows: pl.BlockSpec((rows, BLOCK), lambda k: (0, k))
    specs = [x_spec, along(state_size), along(head_count), along(head_count)]
    operands = [x, write, step, decay]
    if by_head:
        specs.append(pl.BlockSpec((squares.shape[0] // blocks, squares.shape[1]), lambda k: (k, 0)))
        operands.append(squares)
    return pl.pallas_call(
        functools.partial(states_kernel, by_head, features),
        grid=(blocks,),
        in_specs=specs,
        out_specs=[
            pl.BlockSpec((devices, height + TILE, LANES), lambda k: (0, 0, 0)),
            pl.BlockSpec((1, head_count * state_size, LANES), lambda k: (k, 0, 0)),
        ],
        out_shape=[
            jax.ShapeDtypeStruct((devices, height + TILE, LANES), F32),
            jax.ShapeDtypeStruct((blocks, head_count * state_size, LANES), F32),
        ],
        scratch_shapes=[
            pltpu.VMEM((head_count * state_size, LANES), F32),
            pltpu.VMEM((head_count, LANES), F32),
        ],
        compiler_params=params(),
        cost_estimate=pl.CostEstimate(flops=500_000_000, bytes_accessed=6_000_000, transcendentals=20_000),
        name="states",
    )(*operands)


def prefix_kernel(ends_ref, prior_ref):
    devices, height, _ = prior_ref.shape
    running = [jnp.zeros((TILE, LANES), F32) for _ in range(height // TILE)]
    for device in range(devices):
        for tile in range(height // TILE):
            rows = slice(tile * TILE, (tile + 1) * TILE)
            prior_ref[device, rows, :] = running[tile]
            fade = jnp.exp(ends_ref[device, height + tile : height + tile + 1, :])
            running[tile] = fade * running[tile] + ends_ref[device, rows, :]


def prior_states(payload, beside):
    devices, height, _ = payload.shape
    height = height - TILE
    ends = lax.all_to_all(payload, SEQ, split_axis=0, concat_axis=0, tiled=True)
    ends, beside = lax.optimization_barrier((ends, beside))
    prior = pl.pallas_call(
        prefix_kernel,
        out_shape=jax.ShapeDtypeStruct((devices, height, LANES), F32),
        compiler_params=params(8),
        name="prefix",
    )(ends)
    prior = lax.all_to_all(prior, SEQ, split_axis=0, concat_axis=0, tiled=True)
    return prior.reshape(devices * height, LANES), beside


def three_reads(read):
    turned = jnp.transpose(read.astype(F32)).astype(BF16)
    return jnp.concatenate([turned, turned, turned], axis=1)


def read_state(reads, state):
    parts = jnp.concatenate(split_three(state), axis=0)
    return jnp.dot(reads, parts, preferred_element_type=F32)


def local_kernel(by_head, features, *refs):
    if by_head:
        x_ref, write_ref, read_ref, step_ref, decay_ref, squares_ref, before_ref, skip_ref, out_ref, lift_ref, reads_ref, total = refs
    else:
        x_ref, write_ref, read_ref, step_ref, decay_ref, before_ref, skip_ref, out_ref, lift_ref, reads_ref, total = refs
    head_count = step_ref.shape[0]
    state_size = write_ref.shape[0]
    block = pl.program_id(0)
    half = BLOCK // 2

    @pl.when(block == 0)
    def _():
        total[...] = jnp.zeros_like(total)

    cumulative = running_sums(decay_ref[...])
    step = step_ref[...]
    if by_head:
        scale = block_scale(squares_ref, features)
        step = step * scale
        scale_column = jnp.transpose(jnp.broadcast_to(scale, (LANES, BLOCK)))
    padding = jnp.zeros((LANES - head_count, BLOCK), F32)
    columns = jnp.transpose(jnp.concatenate([cumulative, padding], axis=0))
    whole = jnp.concatenate([cumulative + total[:, :1], padding], axis=0)
    lift_ref[...] = jnp.exp(jnp.transpose(whole))
    total[...] = total[...] + jnp.broadcast_to(cumulative[:, BLOCK - 1 :], (head_count, LANES))
    read = read_ref[...]
    reads = three_reads(read)
    reads_ref[...] = reads
    scores = lax.dot_general(read, write_ref[...], (((0,), (0,)), ((), ())), preferred_element_type=F32)
    first, last = slice(0, half), slice(half, BLOCK)
    causal = lax.broadcasted_iota(jnp.int32, (half, half), 0) >= lax.broadcasted_iota(
        jnp.int32, (half, half), 1
    )
    for head in range(head_count):
        row = cumulative[head : head + 1, :]
        column = jnp.broadcast_to(columns[:, head : head + 1], (BLOCK, LANES))
        weight = step[head : head + 1, :]

        def mixing(t, s):
            spread = column[t] - row[:, s]
            if t == s:
                spread = jnp.where(causal, spread, -jnp.inf)
            return (jnp.exp(spread) * scores[t, s] * weight[:, s]).astype(BF16)

        x = head_inputs(x_ref, head, by_head)
        upper = jnp.dot(mixing(first, first), x[first], preferred_element_type=F32)
        both = jnp.concatenate([mixing(last, first), mixing(last, last)], axis=1)
        lower = jnp.dot(both, x, preferred_element_type=F32)
        state = before_ref[0, head * state_size : (head + 1) * state_size, :]
        outputs = jnp.concatenate([upper, lower], axis=0) + jnp.exp(column) * read_state(reads, state)
        skipped = skip_ref[head] * x.astype(F32)
        if by_head:
            skipped = skipped * scale_column
        out_ref[:, head * LANES : (head + 1) * LANES] = outputs + skipped


def local_outputs(x, write, read, step, decay, squares, before, skip, features):
    head_count, length = step.shape
    state_size = write.shape[0]
    blocks = length // BLOCK
    by_head = squares is not None
    if by_head:
        x_spec = pl.BlockSpec((x.shape[0] // blocks, *x.shape[1:]), lambda k: (k, 0, 0))
    else:
        x_spec = pl.BlockSpec((BLOCK, x.shape[1]), lambda k: (k, 0))
    along = lambda rows: pl.BlockSpec((rows, BLOCK), lambda k: (0, k))
    specs = [x_spec, along(state_size), along(state_size), along(head_count), along(head_count)]
    operands = [x, write, read, step, decay]
    if by_head:
        specs.append(pl.BlockSpec((squares.shape[0] // blocks, squares.shape[1]), lambda k: (k, 0)))
        operands.append(squares)
    specs.append(pl.BlockSpec((1, head_count * state_size, LANES), lambda k: (k, 0, 0)))
    specs.append(pl.BlockSpec(memory_space=pltpu.SMEM))
    operands += [before, skip]
    width = head_count * LANES
    return pl.pallas_call(
        functools.partial(local_kernel, by_head, features),
        grid=(blocks,),
        in_specs=specs,
        out_specs=[
            pl.BlockSpec((BLOCK, width), lambda k: (k, 0)),
            pl.BlockSpec((BLOCK, LANES), lambda k: (k, 0)),
            pl.BlockSpec((BLOCK, 3 * state_size), lambda k: (k, 0)),
        ],
        out_shape=[
            jax.ShapeDtypeStruct((length, width), F32),
            jax.ShapeDtypeStruct((length, LANES), F32),
            jax.ShapeDtypeStruct((length, 3 * state_size), BF16),
        ],
        scratch_shapes=[pltpu.VMEM((head_count, LANES), F32)],
        compiler_params=params(),
        cost_estimate=pl.CostEstimate(
            flops=6_000_000_000, bytes_accessed=12_000_000, transcendentals=3_000_000
        ),
        name="local",
    )(*operands)


def gated_kernel(first_layer, groups, local_ref, lift_ref, reads_ref, prior_ref, gate_ref, gain_ref, *refs):
    if first_layer:
        out_ref, total, staged = refs
        cols = out_ref.shape[0]
    else:
        out_ref, squares_ref, total = refs
    group = pl.program_id(0)
    length = local_ref.shape[0]
    heads = local_ref.shape[1] // LANES
    state_size = reads_ref.shape[1] // 3

    @pl.when(group == 0)
    def _():
        total[...] = jnp.zeros_like(total)

    @pl.when(group < groups)
    def _():
        reads = reads_ref[...]
        lifts = pltpu.roll(lift_ref[...], lax.rem(LANES - group * heads, LANES), 1)
        state = prior_ref[...]
        states = [state[head * state_size : (head + 1) * state_size, :] for head in range(heads)]
        from_state = read_state(reads, jnp.concatenate(states, axis=1))
        for head in range(heads):
            place = slice(head * LANES, (head + 1) * LANES)
            outputs = local_ref[:, place] + lifts[:, head : head + 1] * from_state[:, place]
            gate = gate_ref[:, place].astype(F32)
            gated = outputs * (gate / (1.0 + jnp.exp(-gate)))
            total[...] += gated * gated
            gated = gated * gain_ref[:, place]
            if first_layer:
                rows = length // cols
                staged[...] = gated
                for col in range(cols):
                    picked = staged[pl.ds(col, rows, stride=cols), :]
                    out_ref[col, head * rows : (head + 1) * rows, :] = picked.astype(BF16)
            else:
                out_ref[:, place] = gated

    @pl.when(group == pl.num_programs(0) - 1)
    def _():
        ordered = total[...]
        if first_layer:
            rows = length // cols
            ordered = jnp.concatenate(
                [total[pl.ds(col, rows, stride=cols), :] for col in range(cols)], axis=0
            )
        ones = jnp.ones((TILE, LANES), BF16)
        sums = jnp.zeros((TILE, length), F32)
        for part in split_three(ordered):
            sums = sums + lax.dot_general(
                ones, part, (((1,), (1,)), ((), ())), preferred_element_type=F32
            )
        if first_layer:
            high, middle, low = [part.astype(F32) for part in split_three(sums)]
            row = lax.broadcasted_iota(jnp.int32, (TILE, length), 0)
            parts = jnp.where(row == 0, high, jnp.where(row == 1, middle, low))
            parts = jnp.where(row < 3, parts, 0.0)
            empty = jnp.zeros((EXTRA - TILE, LANES), F32)
            for col in range(cols):
                start = col * rows
                inside = start % LANES
                tile = parts[:, start - inside : start - inside + LANES]
                if inside:
                    tile = pltpu.roll(tile, LANES - inside, 1)
                out_ref[col, :EXTRA, :] = jnp.concatenate([tile, empty], axis=0).astype(BF16)
        else:
            squares_ref[...] = sums[:1]


def gated_outputs(first_layer, local, lift, reads, prior, gate, gain, cols):
    length, width = local.shape
    heads = HEADS_PER_STEP
    part = heads * LANES
    groups = width // part
    state_size = reads.shape[1] // 3
    at = lambda g: jnp.minimum(g, groups - 1)
    if first_layer:
        rows = length // cols
        out_specs = pl.BlockSpec((cols, heads * rows, LANES), lambda g: (0, g, 0))
        out_shape = jax.ShapeDtypeStruct((cols, width // LANES * rows + EXTRA, LANES), BF16)
        scratch = [pltpu.VMEM((length, LANES), F32), pltpu.VMEM((length, LANES), F32)]
    else:
        out_specs = [
            pl.BlockSpec((length, part), lambda g: (0, g)),
            pl.BlockSpec((1, length), lambda g: (0, 0)),
        ]
        out_shape = [
            jax.ShapeDtypeStruct((length, width), F32),
            jax.ShapeDtypeStruct((1, length), F32),
        ]
        scratch = [pltpu.VMEM((length, LANES), F32)]
    return pl.pallas_call(
        functools.partial(gated_kernel, first_layer, groups),
        grid=(groups + 1 if first_layer else groups,),
        in_specs=[
            pl.BlockSpec((length, part), lambda g: (0, at(g))),
            pl.BlockSpec((length, LANES), lambda g: (0, 0)),
            pl.BlockSpec((length, 3 * state_size), lambda g: (0, 0)),
            pl.BlockSpec((heads * state_size, LANES), lambda g: (at(g), 0)),
            pl.BlockSpec((length, part), lambda g: (0, at(g))),
            pl.BlockSpec((1, part), lambda g: (0, at(g))),
        ],
        out_specs=out_specs,
        out_shape=out_shape,
        scratch_shapes=scratch,
        compiler_params=params(52),
        cost_estimate=pl.CostEstimate(
            flops=1_200_000_000, bytes_accessed=13_000_000, transcendentals=2_000_000
        ),
        name="gated",
    )(local, lift, reads, prior, gate, gain)


def scaled_kernel(features, gated_ref, squares_ref, out_ref):
    scale = norm_scale(squares_ref[...], features)
    column = jnp.transpose(jnp.broadcast_to(scale, (LANES, scale.shape[1])))
    for head in range(gated_ref.shape[1] // LANES):
        place = slice(head * LANES, (head + 1) * LANES)
        out_ref[:, place] = (gated_ref[:, place] * column).astype(BF16)


def scaled_outputs(gated, squares, features):
    length, width = gated.shape
    return pl.pallas_call(
        functools.partial(scaled_kernel, features),
        grid=(length // BLOCK,),
        in_specs=[
            pl.BlockSpec((BLOCK, width), lambda k: (k, 0)),
            pl.BlockSpec((1, BLOCK), lambda k: (0, k)),
        ],
        out_specs=pl.BlockSpec((BLOCK, width), lambda k: (k, 0)),
        out_shape=jax.ShapeDtypeStruct((length, width), BF16),
        compiler_params=params(),
        name="scaled",
    )(gated, squares)


def body(
    tokens_in,
    gate_rows,
    gate_cols,
    write_rows,
    read_rows,
    step_rows,
    decay_rows,
    skip_rows,
    norm_rows,
    write_cols,
    read_cols,
    step_cols,
    decay_cols,
    skip_cols,
    norm_cols,
):
    grid_rows, grid_cols, width = tokens_in.shape
    devices = lax.axis_size(SEQ)
    features = float(width * lax.axis_size("head"))
    tokens = grid_rows * grid_cols
    column_len = gate_cols.shape[0]

    x = tokens_in.reshape(tokens, width)
    payload, before = device_states(x, write_rows, step_rows, decay_rows, None, features, devices)
    local = local_outputs(
        x, write_rows, read_rows, step_rows, decay_rows, None, before, skip_rows, features
    )
    prior, local = prior_states(payload, local)
    hidden = gated_outputs(
        True, *local, prior, gate_rows.reshape(tokens, width), norm_rows[None], grid_cols
    )
    hidden = lax.all_to_all(hidden, SEQ, split_axis=0, concat_axis=0, tiled=True)
    squares = hidden[:, -EXTRA : 3 - EXTRA, :grid_rows].astype(F32)
    squares = lax.psum(squares[:, 0] + squares[:, 1] + squares[:, 2], "head")

    payload, before = device_states(
        hidden, write_cols, step_cols, decay_cols, squares, features, devices
    )
    local = local_outputs(
        hidden, write_cols, read_cols, step_cols, decay_cols, squares, before, skip_cols, features
    )
    prior, local = prior_states(payload, local)
    gated, squares = gated_outputs(
        False, *local, prior, gate_cols.reshape(column_len, width), norm_cols[None], 1
    )
    squares = lax.psum(squares, "head")
    out = scaled_outputs(gated, squares, features)
    return out.reshape(column_len, 1, width)


def solution(mesh):
    torus = Mesh(
        mesh.devices.reshape(4, 4, 2, mesh.shape["head"]), ("seq_0", "seq_1", "seq_2", "head")
    )
    return jax.shard_map(
        body,
        mesh=torus,
        in_specs=(
            P(SEQ, None, "head"),
            P(SEQ, None, "head"),
            P(None, SEQ, "head"),
            P(None, SEQ),
            P(None, SEQ),
            P("head", SEQ),
            P("head", SEQ),
            P("head"),
            P("head"),
            P(None, SEQ),
            P(None, SEQ),
            P("head", SEQ),
            P("head", SEQ),
            P("head"),
            P("head"),
        ),
        out_specs=P(None, SEQ, "head"),
        check_vma=False,
    )
```

```python
import functools

import jax
import jax.numpy as jnp
from jax import lax
from jax.experimental import pallas as pl
from jax.experimental.pallas import tpu as pltpu
from jax.sharding import Mesh
from jax.sharding import PartitionSpec as P

BLOCK = 256
SEQ = ("seq_0", "seq_1", "seq_2")
EPSILON = 1e-05
LANES = 128
TILE = 8
HEADS_PER_STEP = 2
EXTRA = 16
CHUNK = 128
PITCH = 40
OWN_TYPE = jnp.float32
FACTOR_TYPE = jnp.bfloat16
LAST_TYPE = jnp.float32
SCALED_ROWS = 128
STATES_MB = (56, 48)
MEGABYTE = 1024 * 1024
F32 = jnp.float32
BF16 = jnp.bfloat16


def params(megabytes=56):
    return pltpu.CompilerParams(vmem_limit_bytes=megabytes * MEGABYTE)


def split_three(value):
    high = value.astype(BF16)
    rest = value - high.astype(F32)
    middle = rest.astype(BF16)
    low = (rest - middle.astype(F32)).astype(BF16)
    return high, middle, low


def split_two(value):
    high = value.astype(BF16)
    return high, (value - high.astype(F32)).astype(BF16)


def running_sums(decay):
    length = decay.shape[1]
    earlier = lax.broadcasted_iota(jnp.int32, (length, length), 0)
    later = lax.broadcasted_iota(jnp.int32, (length, length), 1)
    upper = jnp.where(earlier <= later, 1.0, 0.0).astype(BF16)
    high, middle, low = split_three(decay)
    total = jnp.dot(low, upper, preferred_element_type=F32)
    total = total + jnp.dot(middle, upper, preferred_element_type=F32)
    return total + jnp.dot(high, upper, preferred_element_type=F32)


def norm_scale(squares, features):
    return lax.rsqrt(squares / features + EPSILON)


def head_inputs(x_ref, head, by_head):
    if by_head:
        rows = BLOCK // x_ref.shape[0]
        return x_ref[:, head * rows : (head + 1) * rows, :].reshape(BLOCK, LANES)
    return x_ref[:, head * LANES : (head + 1) * LANES]


def block_scale(squares_ref, features):
    squares = squares_ref[...]
    pieces = [squares[device : device + 1, :] for device in range(squares.shape[0])]
    return norm_scale(jnp.concatenate(pieces, axis=1), features)


HBM = pl.BlockSpec(memory_space=pltpu.HBM)
VMEM = pl.BlockSpec(memory_space=pltpu.VMEM)


def silu(value):
    below = 1.0 + jnp.exp(-value)
    inverse = pl.reciprocal(below, approx=True)
    return value * (inverse * (2.0 - below * inverse))


def states_kernel(by_head, features, x_ref, write_hbm, step_hbm, decay_hbm, *refs):
    if by_head:
        squares_ref, gain_ref, payload_hbm, before_hbm, write_ref, step_ref, decay_ref, before, payload, total, sent, got = refs
    else:
        payload_hbm, before_hbm, x_in, write_ref, step_ref, decay_ref, before, payload, total, sent, got = refs
    head_count = step_ref.shape[0]
    state_size = write_ref.shape[0]
    blocks = before.shape[0] - 1
    pairs = ((decay_hbm, decay_ref), (step_hbm, step_ref), (write_hbm, write_ref))
    small = [pltpu.make_async_copy(*pair, got.at[at]) for at, pair in enumerate(pairs)]

    def x_copy(block):
        rows = pl.ds(pl.multiple_of(block * BLOCK, BLOCK), BLOCK)
        return pltpu.make_async_copy(x_ref.at[rows], x_in.at[block], got.at[3 + block])

    def before_copy(block):
        return pltpu.make_async_copy(before.at[block], before_hbm.at[block], sent.at[block])

    for copy in small:
        copy.start()
    if not by_head:
        for block in range(blocks):
            x_copy(block).start()
    before[0] = jnp.zeros(before.shape[1:], F32)
    total[...] = jnp.zeros_like(total)
    for copy in small:
        copy.wait()

    def advance(block, carry):
        positions = pl.ds(pl.multiple_of(block * BLOCK, BLOCK), BLOCK)
        before_copy(block).start()
        cumulative = running_sums(decay_ref[:, positions])
        final = cumulative[:, BLOCK - 1 :]
        weights = jnp.exp(final - cumulative) * step_ref[:, positions]
        if by_head:
            devices = BLOCK // squares_ref.shape[1]
            at = pl.ds(pl.multiple_of(block * devices, devices), devices)
            weights = weights * block_scale(squares_ref[at, :], features)
            x_block = x_ref.at[at]
        else:
            x_copy(block).wait()
            x_block = x_in.at[block]
        fading = jnp.broadcast_to(jnp.exp(final), (head_count, LANES))
        write = write_ref[:, positions].astype(F32)
        for head in range(head_count):
            loaded = (write * weights[head : head + 1, :]).astype(BF16)
            gained = jnp.dot(loaded, head_inputs(x_block, head, by_head), preferred_element_type=F32)
            if by_head:
                gained = gained * gain_ref[:, head * LANES : (head + 1) * LANES]
            rows = slice(head * state_size, (head + 1) * state_size)
            before[block + 1, rows, :] = fading[head : head + 1, :] * before[block, rows, :] + gained
        total[...] = total[...] + jnp.broadcast_to(final, (head_count, LANES))
        return carry

    lax.fori_loop(0, blocks, advance, 0)
    devices, height = payload.shape[0], payload.shape[1] - TILE
    payload[:, :height, :] = before[blocks].reshape(devices, height, LANES)
    for device in range(devices):
        for tile in range(height // TILE):
            head = (device * height + tile * TILE) // state_size
            payload[device, height + tile : height + tile + 1, :] = total[head : head + 1, :]
        left = height + height // TILE
        payload[device, left:, :] = jnp.zeros((height + TILE - left, LANES), F32)
    out = pltpu.make_async_copy(payload, payload_hbm, sent.at[blocks])
    out.start()
    for block in range(blocks):
        before_copy(block).wait()
    out.wait()


def device_states(x, write, step, decay, squares, gain, features, devices):
    head_count, length = step.shape
    state_size = write.shape[0]
    blocks = length // BLOCK
    height = head_count * state_size // devices
    by_head = squares is not None
    specs = [VMEM if by_head else HBM, HBM, HBM, HBM]
    operands = [x, write, step, decay]
    scratch = []
    if by_head:
        specs += [VMEM, VMEM]
        operands += [squares, gain]
    else:
        scratch.append(pltpu.VMEM((blocks, BLOCK, x.shape[1]), BF16))
    return pl.pallas_call(
        functools.partial(states_kernel, by_head, features),
        in_specs=specs,
        out_specs=[HBM, HBM],
        out_shape=[
            jax.ShapeDtypeStruct((devices, height + TILE, LANES), F32),
            jax.ShapeDtypeStruct((blocks, head_count * state_size, LANES), F32),
        ],
        scratch_shapes=scratch
        + [
            pltpu.VMEM(write.shape, BF16),
            pltpu.VMEM(step.shape, F32),
            pltpu.VMEM(decay.shape, F32),
            pltpu.VMEM((blocks + 1, head_count * state_size, LANES), F32),
            pltpu.VMEM((devices, height + TILE, LANES), F32),
            pltpu.VMEM((head_count, LANES), F32),
            pltpu.SemaphoreType.DMA((blocks + 1,)),
            pltpu.SemaphoreType.DMA((3 + blocks,)),
        ],
        compiler_params=params(STATES_MB[by_head]),
        cost_estimate=pl.CostEstimate(flops=500_000_000, bytes_accessed=6_000_000, transcendentals=20_000),
        name="states",
    )(*operands)


def prefix_kernel(ends_ref, prior_ref):
    devices, height, _ = prior_ref.shape
    running = [jnp.zeros((TILE, LANES), F32) for _ in range(height // TILE)]
    for device in range(devices):
        for tile in range(height // TILE):
            rows = slice(tile * TILE, (tile + 1) * TILE)
            prior_ref[device, rows, :] = running[tile]
            fade = jnp.exp(ends_ref[device, height + tile : height + tile + 1, :])
            running[tile] = fade * running[tile] + ends_ref[device, rows, :]


def prior_states(payload, beside):
    devices, height, _ = payload.shape
    height = height - TILE
    ends = lax.all_to_all(payload, SEQ, split_axis=0, concat_axis=0, tiled=True)
    ends, beside = lax.optimization_barrier((ends, beside))
    prior = pl.pallas_call(
        prefix_kernel,
        out_shape=jax.ShapeDtypeStruct((devices, height, LANES), F32),
        compiler_params=params(8),
        name="prefix",
    )(ends)
    prior = lax.all_to_all(prior, SEQ, split_axis=0, concat_axis=0, tiled=True)
    return prior.reshape(devices * height, LANES), beside


def read_state(reads, state):
    parts = jnp.concatenate(split_two(state), axis=0)
    return jnp.dot(reads, parts, preferred_element_type=F32)


def local_kernel(by_head, features, *refs):
    if by_head:
        x_ref, write_ref, read_ref, step_ref, decay_ref, squares_ref, gain_ref, before_ref, skip_ref, out_ref, total = refs
    else:
        x_ref, write_ref, read_ref, step_ref, decay_ref, before_ref, skip_ref, out_ref, total = refs
    head_count = step_ref.shape[0]
    state_size = write_ref.shape[0]
    block = pl.program_id(0)
    half = BLOCK // 2

    @pl.when(block == 0)
    def _():
        total[...] = jnp.zeros_like(total)

    cumulative = running_sums(decay_ref[...])
    step = step_ref[...]
    if by_head:
        scale = block_scale(squares_ref, features)
        step = step * scale
        scale_column = jnp.transpose(jnp.broadcast_to(scale, (LANES, BLOCK)))
    padding = jnp.zeros((LANES - head_count, BLOCK), F32)
    columns = jnp.transpose(jnp.concatenate([cumulative, padding], axis=0))
    whole = jnp.concatenate([cumulative + total[:, :1], padding], axis=0)
    lift = jnp.exp(jnp.transpose(whole))
    total[...] = total[...] + jnp.broadcast_to(cumulative[:, BLOCK - 1 :], (head_count, LANES))
    read = read_ref[...]
    turned = jnp.transpose(read.astype(F32))
    reads = jnp.concatenate([turned, turned], axis=1).astype(BF16)
    out_ref[:, head_count * LANES :] = jnp.concatenate([lift[:, : LANES - state_size], turned], axis=1)
    scores = lax.dot_general(read, write_ref[...], (((0,), (0,)), ((), ())), preferred_element_type=F32)
    first, last = slice(0, half), slice(half, BLOCK)
    causal = lax.broadcasted_iota(jnp.int32, (half, half), 0) >= lax.broadcasted_iota(
        jnp.int32, (half, half), 1
    )
    for head in range(head_count):
        row = cumulative[head : head + 1, :]
        column = jnp.broadcast_to(columns[:, head : head + 1], (BLOCK, LANES))
        weight = step[head : head + 1, :]

        def mixing(t, s):
            spread = column[t] - row[:, s]
            if t == s:
                spread = jnp.where(causal, spread, -jnp.inf)
            return (jnp.exp(spread) * scores[t, s] * weight[:, s]).astype(BF16)

        x = head_inputs(x_ref, head, by_head)
        upper = jnp.dot(mixing(first, first), x[first], preferred_element_type=F32)
        both = jnp.concatenate([mixing(last, first), mixing(last, last)], axis=1)
        lower = jnp.dot(both, x, preferred_element_type=F32)
        state = before_ref[0, head * state_size : (head + 1) * state_size, :]
        place = slice(head * LANES, (head + 1) * LANES)
        skipped = skip_ref[head] * x.astype(F32)
        outputs = jnp.concatenate([upper, lower], axis=0)
        if by_head:
            outputs = (outputs + skipped * scale_column) * gain_ref[:, place]
        else:
            outputs = outputs + skipped
        out_ref[:, place] = outputs + jnp.exp(column) * read_state(reads, state)


def local_outputs(x, write, read, step, decay, squares, gain, before, skip, features):
    head_count, length = step.shape
    state_size = write.shape[0]
    blocks = length // BLOCK
    by_head = squares is not None
    if by_head:
        x_spec = pl.BlockSpec((x.shape[0] // blocks, *x.shape[1:]), lambda k: (k, 0, 0))
    else:
        x_spec = pl.BlockSpec((BLOCK, x.shape[1]), lambda k: (k, 0))
    along = lambda rows: pl.BlockSpec((rows, BLOCK), lambda k: (0, k))
    specs = [x_spec, along(state_size), along(state_size), along(head_count), along(head_count)]
    operands = [x, write, read, step, decay]
    if by_head:
        specs.append(pl.BlockSpec((squares.shape[0] // blocks, squares.shape[1]), lambda k: (k, 0)))
        specs.append(pl.BlockSpec((1, gain.shape[1]), lambda k: (0, 0)))
        operands += [squares, gain]
    specs.append(pl.BlockSpec((1, head_count * state_size, LANES), lambda k: (k, 0, 0)))
    specs.append(pl.BlockSpec(memory_space=pltpu.SMEM))
    operands += [before, skip]
    width = (head_count + 1) * LANES
    return pl.pallas_call(
        functools.partial(local_kernel, by_head, features),
        grid=(blocks,),
        in_specs=specs,
        out_specs=pl.BlockSpec((BLOCK, width), lambda k: (k, 0)),
        out_shape=jax.ShapeDtypeStruct((length, width), F32),
        scratch_shapes=[pltpu.VMEM((head_count, LANES), F32)],
        compiler_params=params(),
        cost_estimate=pl.CostEstimate(
            flops=6_000_000_000, bytes_accessed=12_000_000, transcendentals=3_000_000
        ),
        name="local",
    )(*operands)


def factors_kernel(local_hbm, gate_hbm, own_hbm, factor_hbm, local_in, side, gate_in, own, own_side, factor, sent, got):
    groups, length, width = local_in.shape
    heads = width // LANES

    def lanes(group):
        return pl.ds(pl.multiple_of(group * width, width), width)

    def local_copy(group):
        return pltpu.make_async_copy(local_hbm.at[:, lanes(group)], local_in.at[group], got.at[group])

    def gate_copy(group):
        return pltpu.make_async_copy(gate_hbm.at[:, lanes(group)], gate_in.at[group], got.at[groups + group])

    def own_copy(group):
        return pltpu.make_async_copy(own.at[group], own_hbm.at[:, lanes(group)], sent.at[group])

    def factor_copy(group):
        return pltpu.make_async_copy(factor.at[group], factor_hbm.at[:, lanes(group)], sent.at[groups + group])

    beside = pl.ds(groups * width, LANES)
    side_copy = pltpu.make_async_copy(local_hbm.at[:, beside], side, got.at[2 * groups])
    own_side_copy = pltpu.make_async_copy(own_side, own_hbm.at[:, beside], sent.at[2 * groups])
    side_copy.start()
    for group in range(groups):
        local_copy(group).start()
        gate_copy(group).start()
    side_copy.wait()
    lane = lax.broadcasted_iota(jnp.int32, (length, LANES), 1)
    reads = jnp.where(lane < LANES // 2, pltpu.roll(side[...], LANES // 2, 1), side[...])
    own_side[...] = reads.astype(own_side.dtype)
    own_side_copy.start()

    def advance(group, carry):
        lifts = pltpu.roll(side[...], lax.rem(LANES - group * heads, LANES), 1)
        local_copy(group).wait()
        gate_copy(group).wait()
        for start in range(0, length, CHUNK):
            chunk = slice(start, start + CHUNK)
            for head in range(heads):
                place = slice(head * LANES, (head + 1) * LANES)
                gate = silu(gate_in[group, chunk, place].astype(F32))
                own[group, chunk, place] = (local_in[group, chunk, place] * gate).astype(own.dtype)
                factor[group, chunk, place] = (lifts[chunk, head : head + 1] * gate).astype(factor.dtype)
        own_copy(group).start()
        factor_copy(group).start()
        return carry

    lax.fori_loop(0, groups, advance, 0)
    own_side_copy.wait()
    for group in range(groups):
        own_copy(group).wait()
        factor_copy(group).wait()


def output_factors(local, gate):
    length, width = gate.shape
    part = HEADS_PER_STEP * LANES
    groups = width // part
    return pl.pallas_call(
        factors_kernel,
        in_specs=[HBM, HBM],
        out_specs=[HBM, HBM],
        out_shape=[
            jax.ShapeDtypeStruct((length, width + LANES), OWN_TYPE),
            jax.ShapeDtypeStruct((length, width), FACTOR_TYPE),
        ],
        scratch_shapes=[
            pltpu.VMEM((groups, length, part), F32),
            pltpu.VMEM((length, LANES), F32),
            pltpu.VMEM((groups, length, part), BF16),
            pltpu.VMEM((groups, length, part), OWN_TYPE),
            pltpu.VMEM((length, LANES), OWN_TYPE),
            pltpu.VMEM((groups, length, part), FACTOR_TYPE),
            pltpu.SemaphoreType.DMA((2 * groups + 1,)),
            pltpu.SemaphoreType.DMA((2 * groups + 1,)),
        ],
        compiler_params=params(),
        cost_estimate=pl.CostEstimate(
            flops=100_000_000, bytes_accessed=20_000_000, transcendentals=3_000_000
        ),
        name="factors",
    )(local, gate)


def gated_kernel(first_layer, own_hbm, factor_hbm, prior_ref, *refs):
    if first_layer:
        out_hbm, own, factor, side, out_in, total, sent, got, staged, extra = refs
        cols = out_hbm.shape[0]
    else:
        out_hbm, squares_ref, own, factor, side, out_in, total, sent, got = refs
    groups, length, width = own.shape
    heads = width // LANES
    state_size = LANES // 2

    def lanes(group):
        return pl.ds(pl.multiple_of(group * width, width), width)

    def own_copy(group):
        return pltpu.make_async_copy(own_hbm.at[:, lanes(group)], own.at[group], got.at[group])

    def factor_copy(group):
        return pltpu.make_async_copy(factor_hbm.at[:, lanes(group)], factor.at[group], got.at[groups + group])

    def out_copy(group):
        if first_layer:
            rows = out_in.shape[2]
            place = out_hbm.at[:, pl.ds(pl.multiple_of(group * rows, rows), rows), :]
        else:
            place = out_hbm.at[:, lanes(group)]
        return pltpu.make_async_copy(out_in.at[group], place, sent.at[group])

    side_copy = pltpu.make_async_copy(own_hbm.at[:, pl.ds(groups * width, LANES)], side, got.at[2 * groups])
    side_copy.start()
    for group in range(groups):
        own_copy(group).start()
        factor_copy(group).start()
    total[...] = jnp.zeros_like(total)
    side_copy.wait()

    def advance(group, carry):
        depth = heads * state_size
        state = prior_ref[pl.ds(pl.multiple_of(group * depth, depth), depth), :]
        states = [state[head * state_size : (head + 1) * state_size, :] for head in range(heads)]
        parts = jnp.concatenate(split_two(jnp.concatenate(states, axis=1)), axis=0)
        own_copy(group).wait()
        factor_copy(group).wait()
        for start in range(0, length, CHUNK):
            chunk = slice(start, start + CHUNK)
            from_state = jnp.dot(side[chunk, :].astype(BF16), parts, preferred_element_type=F32)
            squares = total[chunk, :]
            for head in range(heads):
                place = slice(head * LANES, (head + 1) * LANES)
                gated = own[group, chunk, place].astype(F32)
                gated = gated + factor[group, chunk, place].astype(F32) * from_state[:, place]
                squares = squares + gated * gated
                if first_layer:
                    for row in range(CHUNK // cols):
                        pitched = pl.ds((start // cols + row) * PITCH, cols)
                        staged[head, pitched, :] = gated[row * cols : (row + 1) * cols, :]
                else:
                    out_in[group, chunk, place] = gated.astype(out_in.dtype)
            total[chunk, :] = squares
        if first_layer:
            rows = length // cols
            for head in range(heads):
                for col in range(cols):
                    picked = staged[head, pl.ds(col, rows, stride=PITCH), :]
                    out_in[group, col, head * rows : (head + 1) * rows, :] = picked.astype(BF16)
        out_copy(group).start()
        return carry

    lax.fori_loop(0, groups, advance, 0)
    ordered = total[...]
    if first_layer:
        rows = length // cols
        ordered = jnp.concatenate([total[pl.ds(col, rows, stride=cols), :] for col in range(cols)], axis=0)
    ones = jnp.ones((TILE, LANES), BF16)
    sums = jnp.zeros((TILE, length), F32)
    for part in split_three(ordered):
        sums = sums + lax.dot_general(ones, part, (((1,), (1,)), ((), ())), preferred_element_type=F32)
    if first_layer:
        high, middle, low = [part.astype(F32) for part in split_three(sums)]
        row = lax.broadcasted_iota(jnp.int32, (TILE, length), 0)
        parts = jnp.where(row == 0, high, jnp.where(row == 1, middle, low))
        parts = jnp.where(row < 3, parts, 0.0)
        empty = jnp.zeros((EXTRA - TILE, LANES), F32)
        for col in range(cols):
            start = col * rows
            inside = start % LANES
            tile = parts[:, start - inside : start - inside + LANES]
            if inside:
                tile = pltpu.roll(tile, LANES - inside, 1)
            extra[col, :, :] = jnp.concatenate([tile, empty], axis=0).astype(BF16)
        last = out_hbm.at[:, pl.ds(out_hbm.shape[1] - EXTRA, EXTRA), :]
        extra_copy = pltpu.make_async_copy(extra, last, sent.at[groups])
        extra_copy.start()
        extra_copy.wait()
    else:
        squares_ref[...] = sums[:1]
    for group in range(groups):
        out_copy(group).wait()


def gated_outputs(first_layer, own, factor, prior, cols):
    length, width = factor.shape
    heads = HEADS_PER_STEP
    part = heads * LANES
    groups = width // part
    scratch = [
        pltpu.VMEM((groups, length, part), own.dtype),
        pltpu.VMEM((groups, length, part), factor.dtype),
        pltpu.VMEM((length, LANES), own.dtype),
    ]
    last = [
        pltpu.VMEM((length, LANES), F32),
        pltpu.SemaphoreType.DMA((groups + 1,)),
        pltpu.SemaphoreType.DMA((2 * groups + 1,)),
    ]
    if first_layer:
        rows = length // cols
        out_specs = HBM
        out_shape = jax.ShapeDtypeStruct((cols, width // LANES * rows + EXTRA, LANES), BF16)
        scratch.append(pltpu.VMEM((groups, cols, heads * rows, LANES), BF16))
        last += [pltpu.VMEM((heads, rows * PITCH, LANES), F32), pltpu.VMEM((cols, EXTRA, LANES), BF16)]
    else:
        out_specs = [HBM, VMEM]
        out_shape = [
            jax.ShapeDtypeStruct((length, width), LAST_TYPE),
            jax.ShapeDtypeStruct((1, length), F32),
        ]
        scratch.append(pltpu.VMEM((groups, length, part), LAST_TYPE))
    return pl.pallas_call(
        functools.partial(gated_kernel, first_layer),
        in_specs=[HBM, HBM, VMEM],
        out_specs=out_specs,
        out_shape=out_shape,
        scratch_shapes=scratch + last,
        compiler_params=params(52),
        cost_estimate=pl.CostEstimate(
            flops=1_200_000_000, bytes_accessed=13_000_000, transcendentals=2_000_000
        ),
        name="gated",
    )(own, factor, prior)


def scaled_kernel(features, gated_hbm, squares_ref, gain_ref, out_hbm, gated_in, out_in, sent, got):
    parts, rows, width = gated_in.shape

    def gated_copy(part):
        place = pl.ds(pl.multiple_of(part * rows, rows), rows)
        return pltpu.make_async_copy(gated_hbm.at[place], gated_in.at[part], got.at[part])

    def out_copy(part):
        place = pl.ds(pl.multiple_of(part * rows, rows), rows)
        return pltpu.make_async_copy(out_in.at[part], out_hbm.at[place], sent.at[part])

    for part in range(parts):
        gated_copy(part).start()

    def advance(part, carry):
        squares = squares_ref[:, pl.ds(pl.multiple_of(part * rows, rows), rows)]
        scale = norm_scale(squares, features)
        column = jnp.transpose(jnp.broadcast_to(scale, (LANES, rows)))
        gated_copy(part).wait()
        for head in range(width // LANES):
            place = slice(head * LANES, (head + 1) * LANES)
            gated = gated_in[part, :, place].astype(F32) * column
            out_in[part, :, place] = (gated * gain_ref[:, place]).astype(BF16)
        out_copy(part).start()
        return carry

    lax.fori_loop(0, parts, advance, 0)
    for part in range(parts):
        out_copy(part).wait()


def scaled_outputs(gated, squares, gain, features):
    length, width = gated.shape
    parts = length // SCALED_ROWS
    return pl.pallas_call(
        functools.partial(scaled_kernel, features),
        in_specs=[HBM, VMEM, VMEM],
        out_specs=HBM,
        out_shape=jax.ShapeDtypeStruct((length, width), BF16),
        scratch_shapes=[
            pltpu.VMEM((parts, SCALED_ROWS, width), gated.dtype),
            pltpu.VMEM((parts, SCALED_ROWS, width), BF16),
            pltpu.SemaphoreType.DMA((parts,)),
            pltpu.SemaphoreType.DMA((parts,)),
        ],
        compiler_params=params(),
        name="scaled",
    )(gated, squares, gain)


def body(
    tokens_in,
    gate_rows,
    gate_cols,
    write_rows,
    read_rows,
    step_rows,
    decay_rows,
    skip_rows,
    norm_rows,
    write_cols,
    read_cols,
    step_cols,
    decay_cols,
    skip_cols,
    norm_cols,
):
    grid_rows, grid_cols, width = tokens_in.shape
    devices = lax.axis_size(SEQ)
    features = float(width * lax.axis_size("head"))
    tokens = grid_rows * grid_cols
    column_len = gate_cols.shape[0]

    x = tokens_in.reshape(tokens, width)
    payload, before = device_states(x, write_rows, step_rows, decay_rows, None, None, features, devices)
    local = local_outputs(
        x, write_rows, read_rows, step_rows, decay_rows, None, None, before, skip_rows, features
    )
    prior, local = prior_states(payload, local)
    hidden = gated_outputs(
        True, *output_factors(local, gate_rows.reshape(tokens, width)), prior, grid_cols
    )
    hidden = lax.all_to_all(hidden, SEQ, split_axis=0, concat_axis=0, tiled=True)
    squares = hidden[:, -EXTRA : 3 - EXTRA, :grid_rows].astype(F32)
    squares = lax.psum(squares[:, 0] + squares[:, 1] + squares[:, 2], "head")

    payload, before = device_states(
        hidden, write_cols, step_cols, decay_cols, squares, norm_rows[None], features, devices
    )
    local = local_outputs(
        hidden, write_cols, read_cols, step_cols, decay_cols, squares, norm_rows[None], before, skip_cols, features
    )
    prior, local = prior_states(payload, local)
    gated, squares = gated_outputs(
        False, *output_factors(local, gate_cols.reshape(column_len, width)), prior, 1
    )
    squares = lax.psum(squares, "head")
    out = scaled_outputs(gated, squares, norm_cols[None], features)
    return out.reshape(column_len, 1, width)


def solution(mesh):
    torus = Mesh(
        mesh.devices.reshape(4, 4, 2, mesh.shape["head"]), ("seq_0", "seq_1", "seq_2", "head")
    )
    return jax.shard_map(
        body,
        mesh=torus,
        in_specs=(
            P(SEQ, None, "head"),
            P(SEQ, None, "head"),
            P(None, SEQ, "head"),
            P(None, SEQ),
            P(None, SEQ),
            P("head", SEQ),
            P("head", SEQ),
            P("head"),
            P("head"),
            P(None, SEQ),
            P(None, SEQ),
            P("head", SEQ),
            P("head", SEQ),
            P("head"),
            P("head"),
        ),
        out_specs=P(None, SEQ, "head"),
        check_vma=False,
    )
```

```python
import functools

import jax
import jax.numpy as jnp
from jax import lax
from jax.experimental import pallas as pl
from jax.experimental.pallas import tpu as pltpu
from jax.sharding import Mesh
from jax.sharding import PartitionSpec as P

BLOCK = 256
SEQ = ("seq_0", "seq_1", "seq_2")
EPSILON = 1e-05
LANES = 128
TILE = 8
HEADS_PER_STEP = 2
EXTRA = 16
CHUNK = 128
PITCH = 40
LOG2E = 1.4426950408889634
OWN_TYPE = jnp.float32
FACTOR_TYPE = jnp.bfloat16
LAST_TYPE = jnp.bfloat16
SCALED_ROWS = 128
GATED_MB = (49, 52)
MEGABYTE = 1024 * 1024
F32 = jnp.float32
BF16 = jnp.bfloat16


def params(megabytes=56):
    return pltpu.CompilerParams(vmem_limit_bytes=megabytes * MEGABYTE)


def split_three(value):
    high = value.astype(BF16)
    rest = value - high.astype(F32)
    middle = rest.astype(BF16)
    low = (rest - middle.astype(F32)).astype(BF16)
    return high, middle, low


def split_two(value):
    high = value.astype(BF16)
    return high, (value - high.astype(F32)).astype(BF16)


def running_sums(decay):
    length = decay.shape[1]
    earlier = lax.broadcasted_iota(jnp.int32, (length, length), 0)
    later = lax.broadcasted_iota(jnp.int32, (length, length), 1)
    upper = jnp.where(earlier <= later, 1.0, 0.0).astype(BF16)
    high, middle, low = split_three(decay)
    total = jnp.dot(low, upper, preferred_element_type=F32)
    total = total + jnp.dot(middle, upper, preferred_element_type=F32)
    return total + jnp.dot(high, upper, preferred_element_type=F32)


def norm_scale(squares, features):
    return lax.rsqrt(squares / features + EPSILON)


def head_inputs(x_ref, head, by_head):
    if by_head:
        rows = BLOCK // x_ref.shape[0]
        return x_ref[:, head * rows : (head + 1) * rows, :].reshape(BLOCK, LANES)
    return x_ref[:, head * LANES : (head + 1) * LANES]


def block_scale(squares_ref, block, features):
    rows = BLOCK // LANES
    squares = squares_ref[pl.ds(block * rows, rows), :]
    pieces = [squares[row : row + 1, :] for row in range(rows)]
    return norm_scale(jnp.concatenate(pieces, axis=1), features)


HBM = pl.BlockSpec(memory_space=pltpu.HBM)
VMEM = pl.BlockSpec(memory_space=pltpu.VMEM)


def silu(value):
    return value * pl.reciprocal(1.0 + jnp.exp(-value), approx=True)


def states_kernel(by_head, features, x_ref, write_hbm, step_hbm, decay_hbm, *refs):
    if by_head:
        squares_ref, gain_hbm, payload_hbm, before_hbm, gain_ref, x_in, write_ref, step_ref, decay_ref, before, payload, total, sent, got = refs
    else:
        payload_hbm, before_hbm, x_in, write_ref, step_ref, decay_ref, before, payload, total, sent, got = refs
    head_count = step_ref.shape[0]
    state_size = write_ref.shape[0]
    blocks = before.shape[0] - 1
    pairs = ((decay_hbm, decay_ref), (step_hbm, step_ref), (write_hbm, write_ref))
    if by_head:
        pairs += ((gain_hbm, gain_ref),)
    small = [pltpu.make_async_copy(*pair, got.at[at]) for at, pair in enumerate(pairs)]

    def x_copy(block):
        rows = x_in.shape[1]
        place = pl.ds(pl.multiple_of(block * rows, rows), rows)
        return pltpu.make_async_copy(x_ref.at[place], x_in.at[block], got.at[len(pairs) + block])

    def before_copy(block):
        return pltpu.make_async_copy(before.at[block], before_hbm.at[block], sent.at[block])

    for copy in small:
        copy.start()
    for block in range(blocks):
        x_copy(block).start()
    before[0] = jnp.zeros(before.shape[1:], F32)
    total[...] = jnp.zeros_like(total)
    for copy in small:
        copy.wait()

    def advance(block, carry):
        positions = pl.ds(pl.multiple_of(block * BLOCK, BLOCK), BLOCK)
        before_copy(block).start()
        cumulative = running_sums(decay_ref[:, positions])
        final = cumulative[:, BLOCK - 1 :]
        weights = jnp.exp(final - cumulative) * step_ref[:, positions]
        if by_head:
            weights = weights * block_scale(squares_ref, block, features)
        x_copy(block).wait()
        x_block = x_in.at[block]
        fading = jnp.broadcast_to(jnp.exp(final), (head_count, LANES))
        write = write_ref[:, positions].astype(F32)
        for head in range(head_count):
            loaded = (write * weights[head : head + 1, :]).astype(BF16)
            gained = jnp.dot(loaded, head_inputs(x_block, head, by_head), preferred_element_type=F32)
            if by_head:
                gained = gained * gain_ref[:, head * LANES : (head + 1) * LANES]
            rows = slice(head * state_size, (head + 1) * state_size)
            before[block + 1, rows, :] = fading[head : head + 1, :] * before[block, rows, :] + gained
        total[...] = total[...] + jnp.broadcast_to(final, (head_count, LANES))
        return carry

    lax.fori_loop(0, blocks, advance, 0)
    devices, height = payload.shape[0], payload.shape[1] - TILE
    payload[:, :height, :] = before[blocks].reshape(devices, height, LANES)
    for device in range(devices):
        for tile in range(height // TILE):
            head = (device * height + tile * TILE) // state_size
            payload[device, height + tile : height + tile + 1, :] = total[head : head + 1, :]
        left = height + height // TILE
        payload[device, left:, :] = jnp.zeros((height + TILE - left, LANES), F32)
    out = pltpu.make_async_copy(payload, payload_hbm, sent.at[blocks])
    out.start()
    for block in range(blocks):
        before_copy(block).wait()
    out.wait()


def device_states(x, write, step, decay, squares, gain, features, devices):
    head_count, length = step.shape
    state_size = write.shape[0]
    blocks = length // BLOCK
    height = head_count * state_size // devices
    by_head = squares is not None
    specs = [HBM] * 4
    operands = [x, write, step, decay]
    scratch = []
    if by_head:
        specs += [VMEM, HBM]
        operands += [squares, gain]
        scratch.append(pltpu.VMEM(gain.shape, F32))
    scratch.append(pltpu.VMEM((blocks, x.shape[0] // blocks, *x.shape[1:]), BF16))
    return pl.pallas_call(
        functools.partial(states_kernel, by_head, features),
        in_specs=specs,
        out_specs=[HBM, HBM],
        out_shape=[
            jax.ShapeDtypeStruct((devices, height + TILE, LANES), F32),
            jax.ShapeDtypeStruct((blocks, head_count * state_size, LANES), F32),
        ],
        scratch_shapes=scratch
        + [
            pltpu.VMEM(write.shape, BF16),
            pltpu.VMEM(step.shape, F32),
            pltpu.VMEM(decay.shape, F32),
            pltpu.VMEM((blocks + 1, head_count * state_size, LANES), F32),
            pltpu.VMEM((devices, height + TILE, LANES), F32),
            pltpu.VMEM((head_count, LANES), F32),
            pltpu.SemaphoreType.DMA((blocks + 1,)),
            pltpu.SemaphoreType.DMA((4 + blocks,)),
        ],
        compiler_params=params(),
        cost_estimate=pl.CostEstimate(flops=500_000_000, bytes_accessed=6_000_000, transcendentals=20_000),
        name="states",
    )(*operands)


def prefix_kernel(ends_ref, prior_ref):
    devices, height, _ = prior_ref.shape
    running = [jnp.zeros((TILE, LANES), F32) for _ in range(height // TILE)]
    for device in range(devices):
        for tile in range(height // TILE):
            rows = slice(tile * TILE, (tile + 1) * TILE)
            prior_ref[device, rows, :] = running[tile]
            fade = jnp.exp(ends_ref[device, height + tile : height + tile + 1, :])
            running[tile] = fade * running[tile] + ends_ref[device, rows, :]


def prior_states(payload, beside, later):
    devices, height, _ = payload.shape
    height = height - TILE
    ends = lax.all_to_all(payload, SEQ, split_axis=0, concat_axis=0, tiled=True)
    ends, beside, later = lax.optimization_barrier((ends, beside, later))
    prior = pl.pallas_call(
        prefix_kernel,
        out_shape=jax.ShapeDtypeStruct((devices, height, LANES), F32),
        compiler_params=params(8),
        name="prefix",
    )(ends)
    prior = lax.all_to_all(prior, SEQ, split_axis=0, concat_axis=0, tiled=True)
    return prior.reshape(devices * height, LANES), beside, later


def read_state(reads, state):
    parts = jnp.concatenate(split_two(state), axis=0)
    return jnp.dot(reads, parts, preferred_element_type=F32)


def local_kernel(by_head, features, first, *refs):
    x_ref, write_ref, read_ref, step_ref, decay_ref, gate_ref, before_ref, skip_ref = refs[:8]
    if by_head:
        squares_ref, gain_ref = refs[8:10]
    own_ref, factor_ref, total = refs[-3:]
    head_count = step_ref.shape[0]
    state_size = write_ref.shape[0]
    half = BLOCK // 2
    block = first + pl.program_id(0)

    @pl.when(pl.program_id(0) == 0)
    def _():
        total[...] = jnp.zeros_like(total)
        if first:
            earlier = jnp.sum(decay_ref[:, : first * BLOCK], axis=1, keepdims=True)
            total[...] = jnp.broadcast_to(earlier, total.shape)

    cumulative = running_sums(decay_ref[:, pl.ds(pl.multiple_of(block * BLOCK, BLOCK), BLOCK)])
    step = step_ref[...]
    if by_head:
        scale = block_scale(squares_ref, block, features)
        step = step * scale
        scale_column = jnp.transpose(jnp.broadcast_to(scale, (LANES, BLOCK)))
    padding = jnp.zeros((LANES - head_count, BLOCK), F32)
    columns = jnp.transpose(jnp.concatenate([cumulative, padding], axis=0))
    lifts = jnp.exp(columns)
    columns = columns * LOG2E
    lowered = (cumulative - jnp.log(step)) * LOG2E
    kept = jnp.exp(total[...])
    total[...] = total[...] + jnp.broadcast_to(cumulative[:, BLOCK - 1 :], (head_count, LANES))
    read = read_ref[...]
    turned = jnp.transpose(read.astype(F32))
    reads = jnp.concatenate([turned, turned], axis=1)
    own_ref[:, head_count * LANES :] = reads.astype(own_ref.dtype)
    reads = reads.astype(BF16)
    scores = lax.dot_general(read, write_ref[...], (((0,), (0,)), ((), ())), preferred_element_type=F32)
    first_half, last_half = slice(0, half), slice(half, BLOCK)
    causal = lax.broadcasted_iota(jnp.int32, (half, half), 0) >= lax.broadcasted_iota(
        jnp.int32, (half, half), 1
    )
    for head in range(head_count):
        row = lowered[head : head + 1, :]
        column = jnp.broadcast_to(columns[:, head : head + 1], (BLOCK, LANES))

        def mixing(t, s):
            spread = column[t] - row[:, s]
            if t == s:
                spread = jnp.where(causal, spread, -jnp.inf)
            return (jnp.exp2(spread) * scores[t, s]).astype(BF16)

        x = head_inputs(x_ref, head, by_head)
        upper = jnp.dot(mixing(first_half, first_half), x[first_half], preferred_element_type=F32)
        both = jnp.concatenate([mixing(last_half, first_half), mixing(last_half, last_half)], axis=1)
        lower = jnp.dot(both, x, preferred_element_type=F32)
        state = before_ref[0, head * state_size : (head + 1) * state_size, :]
        place = slice(head * LANES, (head + 1) * LANES)
        skipped = skip_ref[head] * x.astype(F32)
        outputs = jnp.concatenate([upper, lower], axis=0)
        if by_head:
            outputs = (outputs + skipped * scale_column) * gain_ref[:, place]
        else:
            outputs = outputs + skipped
        lift = jnp.broadcast_to(lifts[:, head : head + 1], (BLOCK, LANES))
        outputs = outputs + lift * read_state(reads, state)
        gate = silu(gate_ref[:, place].astype(F32))
        own_ref[:, place] = (outputs * gate).astype(own_ref.dtype)
        factor_ref[:, place] = (lift * kept[head : head + 1, :] * gate).astype(factor_ref.dtype)


def local_factors(first, count, x, write, read, step, decay, gate, squares, gain, before, skip, features, done):
    head_count, length = step.shape
    state_size = write.shape[0]
    blocks = length // BLOCK
    width = head_count * LANES
    by_head = squares is not None
    if by_head:
        x_spec = pl.BlockSpec((x.shape[0] // blocks, *x.shape[1:]), lambda k: (first + k, 0, 0))
    else:
        x_spec = pl.BlockSpec((BLOCK, width), lambda k: (first + k, 0))
    along = lambda rows: pl.BlockSpec((rows, BLOCK), lambda k: (0, first + k))
    specs = [
        x_spec,
        along(state_size),
        along(state_size),
        along(head_count),
        pl.BlockSpec((head_count, length), lambda k: (0, 0)),
        pl.BlockSpec((BLOCK, width), lambda k: (first + k, 0)),
        pl.BlockSpec((1, head_count * state_size, LANES), lambda k: (first + k, 0, 0)),
        pl.BlockSpec(memory_space=pltpu.SMEM),
    ]
    operands = [x, write, read, step, decay, gate, before, skip]
    if by_head:
        specs.append(pl.BlockSpec(squares.shape, lambda k: (0, 0)))
        specs.append(pl.BlockSpec((1, width), lambda k: (0, 0)))
        operands += [squares, gain]
    aliases = {len(operands) + at: at for at in range(len(done))}
    return pl.pallas_call(
        functools.partial(local_kernel, by_head, features, first),
        grid=(count,),
        in_specs=specs + [HBM] * len(done),
        input_output_aliases=aliases,
        out_specs=[
            pl.BlockSpec((BLOCK, width + LANES), lambda k: (first + k, 0)),
            pl.BlockSpec((BLOCK, width), lambda k: (first + k, 0)),
        ],
        out_shape=[
            jax.ShapeDtypeStruct((length, width + LANES), OWN_TYPE),
            jax.ShapeDtypeStruct((length, width), FACTOR_TYPE),
        ],
        scratch_shapes=[pltpu.VMEM((head_count, LANES), F32)],
        compiler_params=params(),
        cost_estimate=pl.CostEstimate(
            flops=3_000_000_000, bytes_accessed=10_000_000, transcendentals=3_000_000
        ),
        name="local",
    )(*operands, *done)


def gated_kernel(first_layer, own_hbm, factor_hbm, prior_ref, *refs):
    if first_layer:
        out_hbm, own, factor, side, out_in, total, sent, got, staged, extra = refs
        cols = out_hbm.shape[0]
    else:
        out_ref, squares_ref, own, factor, side, total, got = refs
    groups, length, width = own.shape
    heads = width // LANES
    state_size = LANES // 2

    def lanes(group):
        return pl.ds(pl.multiple_of(group * width, width), width)

    def in_copies(group):
        own_copy = pltpu.make_async_copy(own_hbm.at[:, lanes(group)], own.at[group], got.at[group])
        at = groups + group
        return own_copy, pltpu.make_async_copy(factor_hbm.at[:, lanes(group)], factor.at[group], got.at[at])

    beside = pl.ds(groups * width, LANES)
    side_copy = pltpu.make_async_copy(own_hbm.at[:, beside], side, got.at[2 * groups])

    def out_copy(group):
        rows = out_in.shape[2]
        place = out_hbm.at[:, pl.ds(pl.multiple_of(group * rows, rows), rows), :]
        return pltpu.make_async_copy(out_in.at[group], place, sent.at[group])

    side_copy.start()
    for group in range(groups):
        for copy in in_copies(group):
            copy.start()
    total[...] = jnp.zeros_like(total)
    side_copy.wait()

    def advance(group, carry):
        depth = heads * state_size
        state = prior_ref[pl.ds(pl.multiple_of(group * depth, depth), depth), :]
        states = [state[head * state_size : (head + 1) * state_size, :] for head in range(heads)]
        parts = jnp.concatenate(split_two(jnp.concatenate(states, axis=1)), axis=0)
        for copy in in_copies(group):
            copy.wait()
        for start in range(0, length, CHUNK):
            chunk = slice(start, start + CHUNK)
            from_state = jnp.dot(side[chunk, :].astype(BF16), parts, preferred_element_type=F32)
            squares = total[chunk, :]
            for head in range(heads):
                place = slice(head * LANES, (head + 1) * LANES)
                gated = own[group, chunk, place].astype(F32)
                gated = gated + factor[group, chunk, place].astype(F32) * from_state[:, place]
                squares = squares + gated * gated
                if first_layer:
                    for row in range(CHUNK // cols):
                        pitched = pl.ds((start // cols + row) * PITCH, cols)
                        staged[head, pitched, :] = gated[row * cols : (row + 1) * cols, :]
                else:
                    out_ref[group, chunk, place] = gated.astype(out_ref.dtype)
            total[chunk, :] = squares
        if first_layer:
            rows = length // cols
            for head in range(heads):
                for col in range(cols):
                    picked = staged[head, pl.ds(col, rows, stride=PITCH), :]
                    out_in[group, col, head * rows : (head + 1) * rows, :] = picked.astype(BF16)
            out_copy(group).start()
        return carry

    lax.fori_loop(0, groups, advance, 0)
    ordered = total[...]
    if first_layer:
        rows = length // cols
        ordered = jnp.concatenate([total[pl.ds(col, rows, stride=cols), :] for col in range(cols)], axis=0)
    ones = jnp.ones((TILE, LANES), BF16)
    sums = jnp.zeros((TILE, length), F32)
    for part in split_three(ordered):
        sums = sums + lax.dot_general(ones, part, (((1,), (1,)), ((), ())), preferred_element_type=F32)
    if first_layer:
        high, middle, low = [part.astype(F32) for part in split_three(sums)]
        row = lax.broadcasted_iota(jnp.int32, (TILE, length), 0)
        parts = jnp.where(row == 0, high, jnp.where(row == 1, middle, low))
        parts = jnp.where(row < 3, parts, 0.0)
        empty = jnp.zeros((EXTRA - TILE, LANES), F32)
        for col in range(cols):
            start = col * rows
            inside = start % LANES
            tile = parts[:, start - inside : start - inside + LANES]
            if inside:
                tile = pltpu.roll(tile, LANES - inside, 1)
            extra[col, :, :] = jnp.concatenate([tile, empty], axis=0).astype(BF16)
        last = out_hbm.at[:, pl.ds(out_hbm.shape[1] - EXTRA, EXTRA), :]
        extra_copy = pltpu.make_async_copy(extra, last, sent.at[groups])
        extra_copy.start()
        extra_copy.wait()
        for group in range(groups):
            out_copy(group).wait()
    else:
        squares_ref[...] = sums[:1]


def gated_outputs(first_layer, own, factor, prior, cols):
    length, width = factor.shape
    heads = HEADS_PER_STEP
    part = heads * LANES
    groups = width // part
    scratch = [
        pltpu.VMEM((groups, length, part), own.dtype),
        pltpu.VMEM((groups, length, part), factor.dtype),
        pltpu.VMEM((length, LANES), own.dtype),
    ]
    total = pltpu.VMEM((length, LANES), F32)
    got = pltpu.SemaphoreType.DMA((2 * groups + 1,))
    if first_layer:
        rows = length // cols
        out_specs = HBM
        out_shape = jax.ShapeDtypeStruct((cols, width // LANES * rows + EXTRA, LANES), BF16)
        scratch += [
            pltpu.VMEM((groups, cols, heads * rows, LANES), BF16),
            total,
            pltpu.SemaphoreType.DMA((groups + 1,)),
            got,
            pltpu.VMEM((heads, rows * PITCH, LANES), F32),
            pltpu.VMEM((cols, EXTRA, LANES), BF16),
        ]
    else:
        out_specs = [VMEM, VMEM]
        out_shape = [
            jax.ShapeDtypeStruct((groups, length, part), LAST_TYPE),
            jax.ShapeDtypeStruct((1, length), F32),
        ]
        scratch += [total, got]
    return pl.pallas_call(
        functools.partial(gated_kernel, first_layer),
        in_specs=[HBM, HBM, VMEM],
        out_specs=out_specs,
        out_shape=out_shape,
        scratch_shapes=scratch,
        compiler_params=params(GATED_MB[first_layer]),
        cost_estimate=pl.CostEstimate(
            flops=1_200_000_000, bytes_accessed=13_000_000, transcendentals=2_000_000
        ),
        name="gated",
    )(own, factor, prior)


def scaled_kernel(features, gated_ref, squares_ref, gain_ref, out_hbm, out_in, sent):
    parts, rows, width = out_in.shape
    part_lanes = gated_ref.shape[2]

    def out_copy(part):
        place = pl.ds(pl.multiple_of(part * rows, rows), rows)
        return pltpu.make_async_copy(out_in.at[part], out_hbm.at[place], sent.at[part])

    def advance(part, carry):
        at = pl.ds(pl.multiple_of(part * rows, rows), rows)
        scale = norm_scale(squares_ref[:, at], features)
        column = jnp.transpose(jnp.broadcast_to(scale, (LANES, rows)))
        for head in range(width // LANES):
            place = slice(head * LANES, (head + 1) * LANES)
            group, inside = divmod(head * LANES, part_lanes)
            gated = gated_ref[group, at, inside : inside + LANES].astype(F32) * column
            out_in[part, :, place] = (gated * gain_ref[:, place]).astype(BF16)
        out_copy(part).start()
        return carry

    lax.fori_loop(0, parts, advance, 0)
    for part in range(parts):
        out_copy(part).wait()


def scaled_outputs(gated, squares, gain, features):
    groups, length, part_lanes = gated.shape
    width = groups * part_lanes
    parts = length // SCALED_ROWS
    return pl.pallas_call(
        functools.partial(scaled_kernel, features),
        in_specs=[VMEM, VMEM, VMEM],
        out_specs=HBM,
        out_shape=jax.ShapeDtypeStruct((length, width), BF16),
        scratch_shapes=[
            pltpu.VMEM((parts, SCALED_ROWS, width), BF16),
            pltpu.SemaphoreType.DMA((parts,)),
        ],
        compiler_params=params(48),
        name="scaled",
    )(gated, squares, gain)


def body(
    tokens_in,
    gate_rows,
    gate_cols,
    write_rows,
    read_rows,
    step_rows,
    decay_rows,
    skip_rows,
    norm_rows,
    write_cols,
    read_cols,
    step_cols,
    decay_cols,
    skip_cols,
    norm_cols,
):
    grid_rows, grid_cols, width = tokens_in.shape
    devices = lax.axis_size(SEQ)
    features = float(width * lax.axis_size("head"))
    tokens = grid_rows * grid_cols
    column_len = gate_cols.shape[0]

    x = tokens_in.reshape(tokens, width)
    payload, before = device_states(x, write_rows, step_rows, decay_rows, None, None, features, devices)
    half = tokens // BLOCK // 2
    gate = gate_rows.reshape(tokens, width)
    local = lambda first, decay, done: local_factors(
        first, half, x, write_rows, read_rows, step_rows, decay, gate, None, None, before, skip_rows, features, done
    )
    prior, done, decay = prior_states(payload, local(0, decay_rows, ()), decay_rows)
    hidden = gated_outputs(True, *local(half, decay, done), prior, grid_cols)
    hidden = lax.all_to_all(hidden, SEQ, split_axis=0, concat_axis=0, tiled=True)
    squares = hidden[:, -EXTRA : 3 - EXTRA, :grid_rows].astype(F32)
    squares = (squares[:, 0] + squares[:, 1] + squares[:, 2]).reshape(-1, LANES)
    squares = lax.psum(squares, "head")

    gain = norm_rows[None]
    payload, before = device_states(
        hidden, write_cols, step_cols, decay_cols, squares, gain, features, devices
    )
    half = column_len // BLOCK // 2
    gate = gate_cols.reshape(column_len, width)
    local = lambda first, decay, done: local_factors(
        first, half, hidden, write_cols, read_cols, step_cols, decay, gate, squares, gain, before, skip_cols, features, done
    )
    prior, done, decay = prior_states(payload, local(0, decay_cols, ()), decay_cols)
    gated, last_squares = gated_outputs(False, *local(half, decay, done), prior, 1)
    last_squares = lax.psum(last_squares, "head")
    out = scaled_outputs(gated, last_squares, norm_cols[None], features)
    return out.reshape(column_len, 1, width)


def solution(mesh):
    torus = Mesh(
        mesh.devices.reshape(4, 4, 2, mesh.shape["head"]), ("seq_0", "seq_1", "seq_2", "head")
    )
    return jax.shard_map(
        body,
        mesh=torus,
        in_specs=(
            P(SEQ, None, "head"),
            P(SEQ, None, "head"),
            P(None, SEQ, "head"),
            P(None, SEQ),
            P(None, SEQ),
            P("head", SEQ),
            P("head", SEQ),
            P("head"),
            P("head"),
            P(None, SEQ),
            P(None, SEQ),
            P("head", SEQ),
            P("head", SEQ),
            P("head"),
            P("head"),
        ),
        out_specs=P(None, SEQ, "head"),
        check_vma=False,
    )
```

```python
import functools

import jax
import jax.numpy as jnp
from jax import lax
from jax.experimental import pallas as pl
from jax.experimental.pallas import tpu as pltpu
from jax.sharding import Mesh
from jax.sharding import PartitionSpec as P

BLOCK = 256
SEQ = ("seq_0", "seq_1", "seq_2")
EPSILON = 1e-05
LANES = 128
TILE = 8
HEADS_PER_STEP = 3
EXTRA = 16
CHUNK = 128
PITCH = 40
LOG2E = 1.4426950408889634
OWN_TYPE = jnp.float32
FACTOR_TYPE = jnp.bfloat16
LAST_TYPE = jnp.bfloat16
SCALED_ROWS = 128
GATED_MB = (49, 52)
MEGABYTE = 1024 * 1024
F32 = jnp.float32
BF16 = jnp.bfloat16


def params(megabytes=56):
    return pltpu.CompilerParams(vmem_limit_bytes=megabytes * MEGABYTE)


def split_three(value):
    high = value.astype(BF16)
    rest = value - high.astype(F32)
    middle = rest.astype(BF16)
    low = (rest - middle.astype(F32)).astype(BF16)
    return high, middle, low


def split_two(value):
    high = value.astype(BF16)
    return high, (value - high.astype(F32)).astype(BF16)


def running_sums(decay):
    length = decay.shape[1]
    earlier = lax.broadcasted_iota(jnp.int32, (length, length), 0)
    later = lax.broadcasted_iota(jnp.int32, (length, length), 1)
    upper = jnp.where(earlier <= later, 1.0, 0.0).astype(BF16)
    high, middle, low = split_three(decay)
    total = jnp.dot(low, upper, preferred_element_type=F32)
    total = total + jnp.dot(middle, upper, preferred_element_type=F32)
    return total + jnp.dot(high, upper, preferred_element_type=F32)


def norm_scale(squares, features):
    return lax.rsqrt(squares / features + EPSILON)


def head_inputs(x_ref, head, by_head):
    if by_head:
        rows = BLOCK // x_ref.shape[0]
        return x_ref[:, head * rows : (head + 1) * rows, :].reshape(BLOCK, LANES)
    return x_ref[:, head * LANES : (head + 1) * LANES]


def block_scale(squares_ref, block, features):
    rows = BLOCK // LANES
    squares = squares_ref[pl.ds(block * rows, rows), :]
    pieces = [squares[row : row + 1, :] for row in range(rows)]
    return norm_scale(jnp.concatenate(pieces, axis=1), features)


HBM = pl.BlockSpec(memory_space=pltpu.HBM)
VMEM = pl.BlockSpec(memory_space=pltpu.VMEM)


def silu(value):
    return value * pl.reciprocal(1.0 + jnp.exp(-value), approx=True)


def states_kernel(by_head, features, x_ref, write_hbm, step_hbm, decay_hbm, *refs):
    if by_head:
        squares_hbm, gain_hbm, payload_hbm, before_hbm, gain_ref, squares_ref, x_in, write_ref, step_ref, decay_ref, before, payload, total, sent, got = refs
    else:
        payload_hbm, before_hbm, x_in, write_ref, step_ref, decay_ref, before, payload, total, sent, got = refs
    head_count = step_ref.shape[0]
    state_size = write_ref.shape[0]
    blocks = before.shape[0] - 1
    pairs = ((decay_hbm, decay_ref), (step_hbm, step_ref), (write_hbm, write_ref))
    if by_head:
        pairs += ((squares_hbm, squares_ref), (gain_hbm, gain_ref))
    small = [pltpu.make_async_copy(*pair, got.at[at]) for at, pair in enumerate(pairs)]

    def x_copy(block):
        rows = x_in.shape[1]
        place = pl.ds(pl.multiple_of(block * rows, rows), rows)
        return pltpu.make_async_copy(x_ref.at[place], x_in.at[block], got.at[len(pairs) + block])

    def before_copy(block):
        return pltpu.make_async_copy(before.at[block], before_hbm.at[block], sent.at[block])

    for copy in small:
        copy.start()
    for block in range(blocks):
        x_copy(block).start()
    before[0] = jnp.zeros(before.shape[1:], F32)
    total[...] = jnp.zeros_like(total)
    for copy in small:
        copy.wait()

    def advance(block, carry):
        positions = pl.ds(pl.multiple_of(block * BLOCK, BLOCK), BLOCK)
        before_copy(block).start()
        cumulative = running_sums(decay_ref[:, positions])
        final = cumulative[:, BLOCK - 1 :]
        weights = jnp.exp(final - cumulative) * step_ref[:, positions]
        if by_head:
            weights = weights * block_scale(squares_ref, block, features)
        x_copy(block).wait()
        x_block = x_in.at[block]
        fading = jnp.broadcast_to(jnp.exp(final), (head_count, LANES))
        write = write_ref[:, positions].astype(F32)
        for head in range(head_count):
            loaded = (write * weights[head : head + 1, :]).astype(BF16)
            gained = jnp.dot(loaded, head_inputs(x_block, head, by_head), preferred_element_type=F32)
            if by_head:
                gained = gained * gain_ref[:, head * LANES : (head + 1) * LANES]
            rows = slice(head * state_size, (head + 1) * state_size)
            before[block + 1, rows, :] = fading[head : head + 1, :] * before[block, rows, :] + gained
        total[...] = total[...] + jnp.broadcast_to(final, (head_count, LANES))
        return carry

    lax.fori_loop(0, blocks, advance, 0)
    devices, height = payload.shape[0], payload.shape[1] - TILE
    payload[:, :height, :] = before[blocks].reshape(devices, height, LANES)
    for device in range(devices):
        for tile in range(height // TILE):
            head = (device * height + tile * TILE) // state_size
            payload[device, height + tile : height + tile + 1, :] = total[head : head + 1, :]
        left = height + height // TILE
        payload[device, left:, :] = jnp.zeros((height + TILE - left, LANES), F32)
    out = pltpu.make_async_copy(payload, payload_hbm, sent.at[blocks])
    out.start()
    for block in range(blocks):
        before_copy(block).wait()
    out.wait()


def device_states(x, write, step, decay, squares, gain, features, devices):
    head_count, length = step.shape
    state_size = write.shape[0]
    blocks = length // BLOCK
    height = head_count * state_size // devices
    by_head = squares is not None
    specs = [HBM] * 4
    operands = [x, write, step, decay]
    scratch = []
    if by_head:
        specs += [HBM, HBM]
        operands += [squares, gain]
        scratch += [pltpu.VMEM(gain.shape, F32), pltpu.VMEM(squares.shape, F32)]
    scratch.append(pltpu.VMEM((blocks, x.shape[0] // blocks, *x.shape[1:]), BF16))
    return pl.pallas_call(
        functools.partial(states_kernel, by_head, features),
        in_specs=specs,
        out_specs=[HBM, HBM],
        out_shape=[
            jax.ShapeDtypeStruct((devices, height + TILE, LANES), F32),
            jax.ShapeDtypeStruct((blocks, head_count * state_size, LANES), F32),
        ],
        scratch_shapes=scratch
        + [
            pltpu.VMEM(write.shape, BF16),
            pltpu.VMEM(step.shape, F32),
            pltpu.VMEM(decay.shape, F32),
            pltpu.VMEM((blocks + 1, head_count * state_size, LANES), F32),
            pltpu.VMEM((devices, height + TILE, LANES), F32),
            pltpu.VMEM((head_count, LANES), F32),
            pltpu.SemaphoreType.DMA((blocks + 1,)),
            pltpu.SemaphoreType.DMA((5 + blocks,)),
        ],
        compiler_params=params(),
        cost_estimate=pl.CostEstimate(flops=500_000_000, bytes_accessed=6_000_000, transcendentals=20_000),
        name="states",
    )(*operands)


def prefix_kernel(ends_ref, prior_ref):
    devices, height, _ = prior_ref.shape
    running = [jnp.zeros((TILE, LANES), F32) for _ in range(height // TILE)]
    for device in range(devices):
        for tile in range(height // TILE):
            rows = slice(tile * TILE, (tile + 1) * TILE)
            prior_ref[device, rows, :] = running[tile]
            fade = jnp.exp(ends_ref[device, height + tile : height + tile + 1, :])
            running[tile] = fade * running[tile] + ends_ref[device, rows, :]


def prior_states(payload, beside, later):
    devices, height, _ = payload.shape
    height = height - TILE
    ends = lax.all_to_all(payload, SEQ, split_axis=0, concat_axis=0, tiled=True)
    ends, beside, later = lax.optimization_barrier((ends, beside, later))
    prior = pl.pallas_call(
        prefix_kernel,
        out_shape=jax.ShapeDtypeStruct((devices, height, LANES), F32),
        compiler_params=params(8),
        name="prefix",
    )(ends)
    prior = lax.all_to_all(prior, SEQ, split_axis=0, concat_axis=0, tiled=True)
    return prior.reshape(devices * height, LANES), beside, later


def read_state(reads, state):
    parts = jnp.concatenate(split_two(state), axis=0)
    return jnp.dot(reads, parts, preferred_element_type=F32)


def local_kernel(by_head, features, first, *refs):
    x_ref, write_ref, read_ref, step_ref, decay_ref, gate_ref, before_ref, skip_ref = refs[:8]
    if by_head:
        squares_ref, gain_ref = refs[8:10]
    own_ref, factor_ref, total = refs[-3:]
    head_count = step_ref.shape[0]
    state_size = write_ref.shape[0]
    half = BLOCK // 2
    block = first + pl.program_id(0)

    @pl.when(pl.program_id(0) == 0)
    def _():
        total[...] = jnp.zeros_like(total)
        if first:
            earlier = jnp.sum(decay_ref[:, : first * BLOCK], axis=1, keepdims=True)
            total[...] = jnp.broadcast_to(earlier, total.shape)

    cumulative = running_sums(decay_ref[:, pl.ds(pl.multiple_of(block * BLOCK, BLOCK), BLOCK)])
    step = step_ref[...]
    if by_head:
        scale = block_scale(squares_ref, block, features)
        step = step * scale
        scale_column = jnp.transpose(jnp.broadcast_to(scale, (LANES, BLOCK)))
    padding = jnp.zeros((LANES - head_count, BLOCK), F32)
    columns = jnp.transpose(jnp.concatenate([cumulative, padding], axis=0))
    lifts = jnp.exp(columns)
    columns = columns * LOG2E
    lowered = (cumulative - jnp.log(step)) * LOG2E
    kept = jnp.exp(total[...])
    total[...] = total[...] + jnp.broadcast_to(cumulative[:, BLOCK - 1 :], (head_count, LANES))
    read = read_ref[...]
    turned = jnp.transpose(read.astype(F32))
    reads = jnp.concatenate([turned, turned], axis=1)
    own_ref[own_ref.shape[0] - 1] = jnp.concatenate([reads] * HEADS_PER_STEP, axis=1).astype(own_ref.dtype)
    reads = reads.astype(BF16)
    scores = lax.dot_general(read, write_ref[...], (((0,), (0,)), ((), ())), preferred_element_type=F32)
    first_half, last_half = slice(0, half), slice(half, BLOCK)
    causal = lax.broadcasted_iota(jnp.int32, (half, half), 0) >= lax.broadcasted_iota(
        jnp.int32, (half, half), 1
    )
    for head in range(head_count):
        row = lowered[head : head + 1, :]
        column = jnp.broadcast_to(columns[:, head : head + 1], (BLOCK, LANES))

        def mixing(t, s):
            spread = column[t] - row[:, s]
            if t == s:
                spread = jnp.where(causal, spread, -jnp.inf)
            return (jnp.exp2(spread) * scores[t, s]).astype(BF16)

        x = head_inputs(x_ref, head, by_head)
        upper = jnp.dot(mixing(first_half, first_half), x[first_half], preferred_element_type=F32)
        both = jnp.concatenate([mixing(last_half, first_half), mixing(last_half, last_half)], axis=1)
        lower = jnp.dot(both, x, preferred_element_type=F32)
        state = before_ref[0, head * state_size : (head + 1) * state_size, :]
        place = slice(head * LANES, (head + 1) * LANES)
        skipped = skip_ref[head] * x.astype(F32)
        outputs = jnp.concatenate([upper, lower], axis=0)
        if by_head:
            outputs = (outputs + skipped * scale_column) * gain_ref[:, place]
        else:
            outputs = outputs + skipped
        lift = jnp.broadcast_to(lifts[:, head : head + 1], (BLOCK, LANES))
        outputs = outputs + lift * read_state(reads, state)
        gate = silu(gate_ref[:, place].astype(F32))
        group, inside = divmod(head, HEADS_PER_STEP)
        inside = slice(inside * LANES, (inside + 1) * LANES)
        own_ref[group, :, inside] = (outputs * gate).astype(own_ref.dtype)
        factor_ref[group, :, inside] = (lift * kept[head : head + 1, :] * gate).astype(factor_ref.dtype)


def local_factors(first, count, x, write, read, step, decay, gate, squares, gain, before, skip, features, done):
    head_count, length = step.shape
    state_size = write.shape[0]
    blocks = length // BLOCK
    width = head_count * LANES
    by_head = squares is not None
    if by_head:
        x_spec = pl.BlockSpec((x.shape[0] // blocks, *x.shape[1:]), lambda k: (first + k, 0, 0))
    else:
        x_spec = pl.BlockSpec((BLOCK, width), lambda k: (first + k, 0))
    along = lambda rows: pl.BlockSpec((rows, BLOCK), lambda k: (0, first + k))
    specs = [
        x_spec,
        along(state_size),
        along(state_size),
        along(head_count),
        pl.BlockSpec((head_count, length), lambda k: (0, 0)),
        pl.BlockSpec((BLOCK, width), lambda k: (first + k, 0)),
        pl.BlockSpec((1, head_count * state_size, LANES), lambda k: (first + k, 0, 0)),
        pl.BlockSpec(memory_space=pltpu.SMEM),
    ]
    operands = [x, write, read, step, decay, gate, before, skip]
    if by_head:
        specs.append(pl.BlockSpec(squares.shape, lambda k: (0, 0)))
        specs.append(pl.BlockSpec((1, width), lambda k: (0, 0)))
        operands += [squares, gain]
    part = HEADS_PER_STEP * LANES
    groups = width // part
    aliases = {len(operands) + at: at for at in range(len(done))}
    return pl.pallas_call(
        functools.partial(local_kernel, by_head, features, first),
        grid=(count,),
        in_specs=specs + [HBM] * len(done),
        input_output_aliases=aliases,
        out_specs=[
            pl.BlockSpec((groups + 1, BLOCK, part), lambda k: (0, first + k, 0)),
            pl.BlockSpec((groups, BLOCK, part), lambda k: (0, first + k, 0)),
        ],
        out_shape=[
            jax.ShapeDtypeStruct((groups + 1, length, part), OWN_TYPE),
            jax.ShapeDtypeStruct((groups, length, part), FACTOR_TYPE),
        ],
        scratch_shapes=[pltpu.VMEM((head_count, LANES), F32)],
        compiler_params=params(),
        cost_estimate=pl.CostEstimate(
            flops=3_000_000_000, bytes_accessed=10_000_000, transcendentals=3_000_000
        ),
        name="local",
    )(*operands, *done)


def gated_kernel(first_layer, own_hbm, factor_hbm, prior_ref, *refs):
    if first_layer:
        out_hbm, own, factor, side, out_in, total, sent, got, staged, extra = refs
        cols = out_hbm.shape[0]
    else:
        out_ref, squares_ref, own, factor, side, total, got = refs
    groups, length, width = own.shape
    heads = width // LANES
    state_size = LANES // 2

    def in_copies(group):
        own_copy = pltpu.make_async_copy(own_hbm.at[group], own.at[group], got.at[group])
        at = groups + group
        return own_copy, pltpu.make_async_copy(factor_hbm.at[group], factor.at[group], got.at[at])

    side_copy = pltpu.make_async_copy(own_hbm.at[groups, :, pl.ds(0, LANES)], side, got.at[2 * groups])

    def out_copy(group):
        rows = out_in.shape[2]
        place = out_hbm.at[:, pl.ds(pl.multiple_of(group * rows, rows), rows), :]
        return pltpu.make_async_copy(out_in.at[group], place, sent.at[group])

    side_copy.start()
    for group in range(groups):
        for copy in in_copies(group):
            copy.start()
    total[...] = jnp.zeros_like(total)
    side_copy.wait()

    def advance(group, carry):
        depth = heads * state_size
        state = prior_ref[pl.ds(pl.multiple_of(group * depth, depth), depth), :]
        states = [state[head * state_size : (head + 1) * state_size, :] for head in range(heads)]
        parts = jnp.concatenate(split_two(jnp.concatenate(states, axis=1)), axis=0)
        for copy in in_copies(group):
            copy.wait()
        for start in range(0, length, CHUNK):
            chunk = slice(start, start + CHUNK)
            from_state = jnp.dot(side[chunk, :].astype(BF16), parts, preferred_element_type=F32)
            squares = total[chunk, :]
            for head in range(heads):
                place = slice(head * LANES, (head + 1) * LANES)
                gated = own[group, chunk, place].astype(F32)
                gated = gated + factor[group, chunk, place].astype(F32) * from_state[:, place]
                squares = squares + gated * gated
                if first_layer:
                    for row in range(CHUNK // cols):
                        pitched = pl.ds((start // cols + row) * PITCH, cols)
                        staged[head, pitched, :] = gated[row * cols : (row + 1) * cols, :]
                else:
                    out_ref[group, chunk, place] = gated.astype(out_ref.dtype)
            total[chunk, :] = squares
        if first_layer:
            rows = length // cols
            for head in range(heads):
                for col in range(cols):
                    picked = staged[head, pl.ds(col, rows, stride=PITCH), :]
                    out_in[group, col, head * rows : (head + 1) * rows, :] = picked.astype(BF16)
            out_copy(group).start()
        return carry

    lax.fori_loop(0, groups, advance, 0)
    ordered = total[...]
    if first_layer:
        rows = length // cols
        ordered = jnp.concatenate([total[pl.ds(col, rows, stride=cols), :] for col in range(cols)], axis=0)
    ones = jnp.ones((TILE, LANES), BF16)
    sums = jnp.zeros((TILE, length), F32)
    for part in split_three(ordered):
        sums = sums + lax.dot_general(ones, part, (((1,), (1,)), ((), ())), preferred_element_type=F32)
    if first_layer:
        high, middle, low = [part.astype(F32) for part in split_three(sums)]
        row = lax.broadcasted_iota(jnp.int32, (TILE, length), 0)
        parts = jnp.where(row == 0, high, jnp.where(row == 1, middle, low))
        parts = jnp.where(row < 3, parts, 0.0)
        empty = jnp.zeros((EXTRA - TILE, LANES), F32)
        for col in range(cols):
            start = col * rows
            inside = start % LANES
            tile = parts[:, start - inside : start - inside + LANES]
            if inside:
                tile = pltpu.roll(tile, LANES - inside, 1)
            extra[col, :, :] = jnp.concatenate([tile, empty], axis=0).astype(BF16)
        last = out_hbm.at[:, pl.ds(out_hbm.shape[1] - EXTRA, EXTRA), :]
        extra_copy = pltpu.make_async_copy(extra, last, sent.at[groups])
        extra_copy.start()
        extra_copy.wait()
        for group in range(groups):
            out_copy(group).wait()
    else:
        squares_ref[...] = sums[:1]


def gated_outputs(first_layer, own, factor, prior, cols):
    groups, length, part = factor.shape
    heads = part // LANES
    width = groups * part
    scratch = [
        pltpu.VMEM((groups, length, part), own.dtype),
        pltpu.VMEM((groups, length, part), factor.dtype),
        pltpu.VMEM((length, LANES), own.dtype),
    ]
    total = pltpu.VMEM((length, LANES), F32)
    got = pltpu.SemaphoreType.DMA((2 * groups + 1,))
    if first_layer:
        rows = length // cols
        out_specs = HBM
        out_shape = jax.ShapeDtypeStruct((cols, width // LANES * rows + EXTRA, LANES), BF16)
        scratch += [
            pltpu.VMEM((groups, cols, heads * rows, LANES), BF16),
            total,
            pltpu.SemaphoreType.DMA((groups + 1,)),
            got,
            pltpu.VMEM((heads, rows * PITCH, LANES), F32),
            pltpu.VMEM((cols, EXTRA, LANES), BF16),
        ]
    else:
        out_specs = [VMEM, VMEM]
        out_shape = [
            jax.ShapeDtypeStruct((groups, length, part), LAST_TYPE),
            jax.ShapeDtypeStruct((1, length), F32),
        ]
        scratch += [total, got]
    return pl.pallas_call(
        functools.partial(gated_kernel, first_layer),
        in_specs=[HBM, HBM, VMEM],
        out_specs=out_specs,
        out_shape=out_shape,
        scratch_shapes=scratch,
        compiler_params=params(GATED_MB[first_layer]),
        cost_estimate=pl.CostEstimate(
            flops=1_200_000_000, bytes_accessed=13_000_000, transcendentals=2_000_000
        ),
        name="gated",
    )(own, factor, prior)


def scaled_kernel(features, gated_ref, squares_ref, gain_ref, out_hbm, out_in, sent):
    parts, rows, width = out_in.shape
    part_lanes = gated_ref.shape[2]

    def out_copy(part):
        place = pl.ds(pl.multiple_of(part * rows, rows), rows)
        return pltpu.make_async_copy(out_in.at[part], out_hbm.at[place], sent.at[part])

    def advance(part, carry):
        at = pl.ds(pl.multiple_of(part * rows, rows), rows)
        scale = norm_scale(squares_ref[:, at], features)
        column = jnp.transpose(jnp.broadcast_to(scale, (LANES, rows)))
        for head in range(width // LANES):
            place = slice(head * LANES, (head + 1) * LANES)
            group, inside = divmod(head * LANES, part_lanes)
            gated = gated_ref[group, at, inside : inside + LANES].astype(F32) * column
            out_in[part, :, place] = (gated * gain_ref[:, place]).astype(BF16)
        out_copy(part).start()
        return carry

    lax.fori_loop(0, parts, advance, 0)
    for part in range(parts):
        out_copy(part).wait()


def scaled_outputs(gated, squares, gain, features):
    groups, length, part_lanes = gated.shape
    width = groups * part_lanes
    parts = length // SCALED_ROWS
    return pl.pallas_call(
        functools.partial(scaled_kernel, features),
        in_specs=[VMEM, VMEM, VMEM],
        out_specs=HBM,
        out_shape=jax.ShapeDtypeStruct((length, width), BF16),
        scratch_shapes=[
            pltpu.VMEM((parts, SCALED_ROWS, width), BF16),
            pltpu.SemaphoreType.DMA((parts,)),
        ],
        compiler_params=params(48),
        name="scaled",
    )(gated, squares, gain)


def sum_over_head(value):
    devices = lax.axis_size("head")
    total = value
    for step in range(1, devices):
        total = total + lax.ppermute(value, "head", [(at, at ^ step) for at in range(devices)])
    return total


def body(
    tokens_in,
    gate_rows,
    gate_cols,
    write_rows,
    read_rows,
    step_rows,
    decay_rows,
    skip_rows,
    norm_rows,
    write_cols,
    read_cols,
    step_cols,
    decay_cols,
    skip_cols,
    norm_cols,
):
    grid_rows, grid_cols, width = tokens_in.shape
    devices = lax.axis_size(SEQ)
    features = float(width * lax.axis_size("head"))
    tokens = grid_rows * grid_cols
    column_len = gate_cols.shape[0]

    x = tokens_in.reshape(tokens, width)
    payload, before = device_states(x, write_rows, step_rows, decay_rows, None, None, features, devices)
    half = tokens // BLOCK // 2
    gate = gate_rows.reshape(tokens, width)
    local = lambda first, decay, done: local_factors(
        first, half, x, write_rows, read_rows, step_rows, decay, gate, None, None, before, skip_rows, features, done
    )
    prior, done, decay = prior_states(payload, local(0, decay_rows, ()), decay_rows)
    hidden = gated_outputs(True, *local(half, decay, done), prior, grid_cols)
    hidden = lax.all_to_all(hidden, SEQ, split_axis=0, concat_axis=0, tiled=True)
    squares = hidden[:, -EXTRA : 3 - EXTRA, :grid_rows].astype(F32)
    squares = (squares[:, 0] + squares[:, 1] + squares[:, 2]).reshape(-1, LANES)
    squares = sum_over_head(squares)

    gain = norm_rows[None]
    payload, before = device_states(
        hidden, write_cols, step_cols, decay_cols, squares, gain, features, devices
    )
    half = column_len // BLOCK // 2
    gate = gate_cols.reshape(column_len, width)
    local = lambda first, decay, done: local_factors(
        first, half, hidden, write_cols, read_cols, step_cols, decay, gate, squares, gain, before, skip_cols, features, done
    )
    prior, done, decay = prior_states(payload, local(0, decay_cols, ()), decay_cols)
    gated, last_squares = gated_outputs(False, *local(half, decay, done), prior, 1)
    last_squares = sum_over_head(last_squares)
    out = scaled_outputs(gated, last_squares, norm_cols[None], features)
    return out.reshape(column_len, 1, width)


def solution(mesh):
    torus = Mesh(
        mesh.devices.reshape(4, 4, 2, mesh.shape["head"]), ("seq_0", "seq_1", "seq_2", "head")
    )
    return jax.shard_map(
        body,
        mesh=torus,
        in_specs=(
            P(SEQ, None, "head"),
            P(SEQ, None, "head"),
            P(None, SEQ, "head"),
            P(None, SEQ),
            P(None, SEQ),
            P("head", SEQ),
            P("head", SEQ),
            P("head"),
            P("head"),
            P(None, SEQ),
            P(None, SEQ),
            P("head", SEQ),
            P("head", SEQ),
            P("head"),
            P("head"),
        ),
        out_specs=P(None, SEQ, "head"),
        check_vma=False,
    )
```

```python
import functools

import jax
import jax.numpy as jnp
from jax import lax
from jax.experimental import pallas as pl
from jax.experimental.pallas import tpu as pltpu
from jax.sharding import Mesh
from jax.sharding import PartitionSpec as P

BLOCK = 256
SEQ = ("seq_0", "seq_1", "seq_2")
EPSILON = 1e-05
LANES = 128
TILE = 8
HEADS_PER_STEP = 3
EXTRA = 16
CHUNK = 128
PITCH = 40
LOG2E = 1.4426950408889634
OWN_TYPE = jnp.float32
FACTOR_TYPE = jnp.bfloat16
LAST_TYPE = jnp.bfloat16
SCALED_ROWS = 128
GATED_MB = (49, 52)
MEGABYTE = 1024 * 1024
F32 = jnp.float32
BF16 = jnp.bfloat16


def params(megabytes=56):
    return pltpu.CompilerParams(vmem_limit_bytes=megabytes * MEGABYTE)


def split_three(value):
    high = value.astype(BF16)
    rest = value - high.astype(F32)
    middle = rest.astype(BF16)
    low = (rest - middle.astype(F32)).astype(BF16)
    return high, middle, low


def split_two(value):
    high = value.astype(BF16)
    return high, (value - high.astype(F32)).astype(BF16)


def running_sums(decay):
    length = decay.shape[1]
    earlier = lax.broadcasted_iota(jnp.int32, (length, length), 0)
    later = lax.broadcasted_iota(jnp.int32, (length, length), 1)
    upper = jnp.where(earlier <= later, 1.0, 0.0).astype(BF16)
    high, middle, low = split_three(decay)
    total = jnp.dot(low, upper, preferred_element_type=F32)
    total = total + jnp.dot(middle, upper, preferred_element_type=F32)
    return total + jnp.dot(high, upper, preferred_element_type=F32)


def norm_scale(squares, features):
    return lax.rsqrt(squares / features + EPSILON)


def head_inputs(x_ref, head, by_head):
    if by_head:
        rows = BLOCK // x_ref.shape[0]
        return x_ref[:, head * rows : (head + 1) * rows, :].reshape(BLOCK, LANES)
    return x_ref[:, head * LANES : (head + 1) * LANES]


def block_scale(squares_refs, block, features):
    rows = BLOCK // LANES
    squares = sum(ref[pl.ds(block * rows, rows), :] for ref in squares_refs)
    pieces = [squares[row : row + 1, :] for row in range(rows)]
    return norm_scale(jnp.concatenate(pieces, axis=1), features)


HBM = pl.BlockSpec(memory_space=pltpu.HBM)
VMEM = pl.BlockSpec(memory_space=pltpu.VMEM)


def silu(value):
    return value * pl.reciprocal(1.0 + jnp.exp(-value), approx=True)


def states_kernel(by_head, features, x_ref, write_hbm, step_hbm, decay_hbm, *refs):
    if by_head:
        *squares_hbms, gain_hbm, payload_hbm, before_hbm, gain_ref, squares_ref, x_in, write_ref, step_ref, decay_ref, before, payload, total, sent, got = refs
    else:
        payload_hbm, before_hbm, x_in, write_ref, step_ref, decay_ref, before, payload, total, sent, got = refs
    head_count = step_ref.shape[0]
    state_size = write_ref.shape[0]
    blocks = before.shape[0] - 1
    pairs = ((decay_hbm, decay_ref), (step_hbm, step_ref), (write_hbm, write_ref))
    if by_head:
        squares_refs = [squares_ref.at[at] for at in range(len(squares_hbms))]
        pairs += ((gain_hbm, gain_ref), *zip(squares_hbms, squares_refs))
    small = [pltpu.make_async_copy(*pair, got.at[at]) for at, pair in enumerate(pairs)]

    def x_copy(block):
        rows = x_in.shape[1]
        place = pl.ds(pl.multiple_of(block * rows, rows), rows)
        return pltpu.make_async_copy(x_ref.at[place], x_in.at[block], got.at[len(pairs) + block])

    def before_copy(block):
        return pltpu.make_async_copy(before.at[block], before_hbm.at[block], sent.at[block])

    for copy in small:
        copy.start()
    for block in range(blocks):
        x_copy(block).start()
    before[0] = jnp.zeros(before.shape[1:], F32)
    total[...] = jnp.zeros_like(total)
    for copy in small:
        copy.wait()

    def advance(block, carry):
        positions = pl.ds(pl.multiple_of(block * BLOCK, BLOCK), BLOCK)
        before_copy(block).start()
        cumulative = running_sums(decay_ref[:, positions])
        final = cumulative[:, BLOCK - 1 :]
        weights = jnp.exp(final - cumulative) * step_ref[:, positions]
        if by_head:
            weights = weights * block_scale(squares_refs, block, features)
        x_copy(block).wait()
        x_block = x_in.at[block]
        fading = jnp.broadcast_to(jnp.exp(final), (head_count, LANES))
        write = write_ref[:, positions].astype(F32)
        for head in range(head_count):
            loaded = (write * weights[head : head + 1, :]).astype(BF16)
            gained = jnp.dot(loaded, head_inputs(x_block, head, by_head), preferred_element_type=F32)
            if by_head:
                gained = gained * gain_ref[:, head * LANES : (head + 1) * LANES]
            rows = slice(head * state_size, (head + 1) * state_size)
            before[block + 1, rows, :] = fading[head : head + 1, :] * before[block, rows, :] + gained
        total[...] = total[...] + jnp.broadcast_to(final, (head_count, LANES))
        return carry

    lax.fori_loop(0, blocks, advance, 0)
    devices, height = payload.shape[0], payload.shape[1] - TILE
    payload[:, :height, :] = before[blocks].reshape(devices, height, LANES)
    for device in range(devices):
        for tile in range(height // TILE):
            head = (device * height + tile * TILE) // state_size
            payload[device, height + tile : height + tile + 1, :] = total[head : head + 1, :]
        left = height + height // TILE
        payload[device, left:, :] = jnp.zeros((height + TILE - left, LANES), F32)
    out = pltpu.make_async_copy(payload, payload_hbm, sent.at[blocks])
    out.start()
    for block in range(blocks):
        before_copy(block).wait()
    out.wait()


def device_states(x, write, step, decay, squares, gain, features, devices):
    head_count, length = step.shape
    state_size = write.shape[0]
    blocks = length // BLOCK
    height = head_count * state_size // devices
    by_head = squares is not None
    specs = [HBM] * 4
    operands = [x, write, step, decay]
    scratch = []
    if by_head:
        specs += [HBM] * (len(squares) + 1)
        operands += [*squares, gain]
        scratch += [pltpu.VMEM(gain.shape, F32), pltpu.VMEM((len(squares), *squares[0].shape), F32)]
    scratch.append(pltpu.VMEM((blocks, x.shape[0] // blocks, *x.shape[1:]), BF16))
    return pl.pallas_call(
        functools.partial(states_kernel, by_head, features),
        in_specs=specs,
        out_specs=[HBM, HBM],
        out_shape=[
            jax.ShapeDtypeStruct((devices, height + TILE, LANES), F32),
            jax.ShapeDtypeStruct((blocks, head_count * state_size, LANES), F32),
        ],
        scratch_shapes=scratch
        + [
            pltpu.VMEM(write.shape, BF16),
            pltpu.VMEM(step.shape, F32),
            pltpu.VMEM(decay.shape, F32),
            pltpu.VMEM((blocks + 1, head_count * state_size, LANES), F32),
            pltpu.VMEM((devices, height + TILE, LANES), F32),
            pltpu.VMEM((head_count, LANES), F32),
            pltpu.SemaphoreType.DMA((blocks + 1,)),
            pltpu.SemaphoreType.DMA((len(operands) + blocks,)),
        ],
        compiler_params=params(),
        cost_estimate=pl.CostEstimate(flops=500_000_000, bytes_accessed=6_000_000, transcendentals=20_000),
        name="states",
    )(*operands)


def prefix_kernel(ends_ref, prior_ref):
    devices, height, _ = prior_ref.shape
    running = [jnp.zeros((TILE, LANES), F32) for _ in range(height // TILE)]
    for device in range(devices):
        for tile in range(height // TILE):
            rows = slice(tile * TILE, (tile + 1) * TILE)
            prior_ref[device, rows, :] = running[tile]
            fade = jnp.exp(ends_ref[device, height + tile : height + tile + 1, :])
            running[tile] = fade * running[tile] + ends_ref[device, rows, :]


def prior_states(payload, beside, later):
    devices, height, _ = payload.shape
    height = height - TILE
    ends = lax.all_to_all(payload, SEQ, split_axis=0, concat_axis=0, tiled=True)
    ends, beside, later = lax.optimization_barrier((ends, beside, later))
    prior = pl.pallas_call(
        prefix_kernel,
        out_shape=jax.ShapeDtypeStruct((devices, height, LANES), F32),
        compiler_params=params(8),
        name="prefix",
    )(ends)
    prior = lax.all_to_all(prior, SEQ, split_axis=0, concat_axis=0, tiled=True)
    return prior.reshape(devices * height, LANES), beside, later


def read_state(reads, state):
    parts = jnp.concatenate(split_two(state), axis=0)
    return jnp.dot(reads, parts, preferred_element_type=F32)


def local_kernel(by_head, features, first, parts, *refs):
    x_ref, write_ref, read_ref, step_ref, decay_ref, gate_ref, before_ref, skip_ref = refs[:8]
    if by_head:
        *squares_refs, gain_ref = refs[8 : 9 + parts]
    own_ref, factor_ref, total = refs[-3:]
    head_count = step_ref.shape[0]
    state_size = write_ref.shape[0]
    half = BLOCK // 2
    block = first + pl.program_id(0)

    @pl.when(pl.program_id(0) == 0)
    def _():
        total[...] = jnp.zeros_like(total)
        if first:
            earlier = jnp.sum(decay_ref[:, : first * BLOCK], axis=1, keepdims=True)
            total[...] = jnp.broadcast_to(earlier, total.shape)

    cumulative = running_sums(decay_ref[:, pl.ds(pl.multiple_of(block * BLOCK, BLOCK), BLOCK)])
    step = step_ref[...]
    if by_head:
        scale = block_scale(squares_refs, block, features)
        step = step * scale
        scale_column = jnp.transpose(jnp.broadcast_to(scale, (LANES, BLOCK)))
    padding = jnp.zeros((LANES - head_count, BLOCK), F32)
    columns = jnp.transpose(jnp.concatenate([cumulative, padding], axis=0))
    lifts = jnp.exp(columns)
    columns = columns * LOG2E
    lowered = (cumulative - jnp.log(step)) * LOG2E
    kept = jnp.exp(total[...])
    total[...] = total[...] + jnp.broadcast_to(cumulative[:, BLOCK - 1 :], (head_count, LANES))
    read = read_ref[...]
    turned = jnp.transpose(read.astype(F32))
    reads = jnp.concatenate([turned, turned], axis=1)
    own_ref[own_ref.shape[0] - 1] = jnp.concatenate([reads] * HEADS_PER_STEP, axis=1).astype(own_ref.dtype)
    reads = reads.astype(BF16)
    scores = lax.dot_general(read, write_ref[...], (((0,), (0,)), ((), ())), preferred_element_type=F32)
    first_half, last_half = slice(0, half), slice(half, BLOCK)
    causal = lax.broadcasted_iota(jnp.int32, (half, half), 0) >= lax.broadcasted_iota(
        jnp.int32, (half, half), 1
    )
    for head in range(head_count):
        row = lowered[head : head + 1, :]
        column = jnp.broadcast_to(columns[:, head : head + 1], (BLOCK, LANES))

        def mixing(t, s):
            spread = column[t] - row[:, s]
            if t == s:
                spread = jnp.where(causal, spread, -jnp.inf)
            return (jnp.exp2(spread) * scores[t, s]).astype(BF16)

        x = head_inputs(x_ref, head, by_head)
        upper = jnp.dot(mixing(first_half, first_half), x[first_half], preferred_element_type=F32)
        both = jnp.concatenate([mixing(last_half, first_half), mixing(last_half, last_half)], axis=1)
        lower = jnp.dot(both, x, preferred_element_type=F32)
        state = before_ref[0, head * state_size : (head + 1) * state_size, :]
        place = slice(head * LANES, (head + 1) * LANES)
        skipped = skip_ref[head] * x.astype(F32)
        outputs = jnp.concatenate([upper, lower], axis=0)
        if by_head:
            outputs = (outputs + skipped * scale_column) * gain_ref[:, place]
        else:
            outputs = outputs + skipped
        lift = jnp.broadcast_to(lifts[:, head : head + 1], (BLOCK, LANES))
        outputs = outputs + lift * read_state(reads, state)
        gate = silu(gate_ref[:, place].astype(F32))
        group, inside = divmod(head, HEADS_PER_STEP)
        inside = slice(inside * LANES, (inside + 1) * LANES)
        own_ref[group, :, inside] = (outputs * gate).astype(own_ref.dtype)
        factor_ref[group, :, inside] = (lift * kept[head : head + 1, :] * gate).astype(factor_ref.dtype)


def local_factors(first, count, x, write, read, step, decay, gate, squares, gain, before, skip, features, done):
    head_count, length = step.shape
    state_size = write.shape[0]
    blocks = length // BLOCK
    width = head_count * LANES
    by_head = squares is not None
    if by_head:
        x_spec = pl.BlockSpec((x.shape[0] // blocks, *x.shape[1:]), lambda k: (first + k, 0, 0))
    else:
        x_spec = pl.BlockSpec((BLOCK, width), lambda k: (first + k, 0))
    along = lambda rows: pl.BlockSpec((rows, BLOCK), lambda k: (0, first + k))
    specs = [
        x_spec,
        along(state_size),
        along(state_size),
        along(head_count),
        pl.BlockSpec((head_count, length), lambda k: (0, 0)),
        pl.BlockSpec((BLOCK, width), lambda k: (first + k, 0)),
        pl.BlockSpec((1, head_count * state_size, LANES), lambda k: (first + k, 0, 0)),
        pl.BlockSpec(memory_space=pltpu.SMEM),
    ]
    operands = [x, write, read, step, decay, gate, before, skip]
    if by_head:
        specs += [pl.BlockSpec(part.shape, lambda k: (0, 0)) for part in squares]
        specs.append(pl.BlockSpec((1, width), lambda k: (0, 0)))
        operands += [*squares, gain]
    part = HEADS_PER_STEP * LANES
    groups = width // part
    aliases = {len(operands) + at: at for at in range(len(done))}
    return pl.pallas_call(
        functools.partial(local_kernel, by_head, features, first, len(squares) if by_head else 0),
        grid=(count,),
        in_specs=specs + [HBM] * len(done),
        input_output_aliases=aliases,
        out_specs=[
            pl.BlockSpec((groups + 1, BLOCK, part), lambda k: (0, first + k, 0)),
            pl.BlockSpec((groups, BLOCK, part), lambda k: (0, first + k, 0)),
        ],
        out_shape=[
            jax.ShapeDtypeStruct((groups + 1, length, part), OWN_TYPE),
            jax.ShapeDtypeStruct((groups, length, part), FACTOR_TYPE),
        ],
        scratch_shapes=[pltpu.VMEM((head_count, LANES), F32)],
        compiler_params=params(),
        cost_estimate=pl.CostEstimate(
            flops=3_000_000_000, bytes_accessed=10_000_000, transcendentals=3_000_000
        ),
        name="local",
    )(*operands, *done)


def gated_kernel(first_layer, own_hbm, factor_hbm, prior_ref, *refs):
    if first_layer:
        out_hbm, own, factor, side, out_in, total, sent, got, staged, extra = refs
        cols = out_hbm.shape[0]
    else:
        out_ref, squares_ref, own, factor, side, total, got = refs
    groups, length, width = own.shape
    heads = width // LANES
    state_size = LANES // 2

    def in_copies(group):
        own_copy = pltpu.make_async_copy(own_hbm.at[group], own.at[group], got.at[group])
        at = groups + group
        return own_copy, pltpu.make_async_copy(factor_hbm.at[group], factor.at[group], got.at[at])

    side_copy = pltpu.make_async_copy(own_hbm.at[groups, :, pl.ds(0, LANES)], side, got.at[2 * groups])

    def out_copy(group):
        rows = out_in.shape[2]
        place = out_hbm.at[:, pl.ds(pl.multiple_of(group * rows, rows), rows), :]
        return pltpu.make_async_copy(out_in.at[group], place, sent.at[group])

    side_copy.start()
    for group in range(groups):
        for copy in in_copies(group):
            copy.start()
    total[...] = jnp.zeros_like(total)
    side_copy.wait()

    def advance(group, carry):
        depth = heads * state_size
        state = prior_ref[pl.ds(pl.multiple_of(group * depth, depth), depth), :]
        states = [state[head * state_size : (head + 1) * state_size, :] for head in range(heads)]
        parts = jnp.concatenate(split_two(jnp.concatenate(states, axis=1)), axis=0)
        for copy in in_copies(group):
            copy.wait()
        for start in range(0, length, CHUNK):
            chunk = slice(start, start + CHUNK)
            from_state = jnp.dot(side[chunk, :].astype(BF16), parts, preferred_element_type=F32)
            squares = total[chunk, :]
            for head in range(heads):
                place = slice(head * LANES, (head + 1) * LANES)
                gated = own[group, chunk, place].astype(F32)
                gated = gated + factor[group, chunk, place].astype(F32) * from_state[:, place]
                squares = squares + gated * gated
                if first_layer:
                    for row in range(CHUNK // cols):
                        pitched = pl.ds((start // cols + row) * PITCH, cols)
                        staged[head, pitched, :] = gated[row * cols : (row + 1) * cols, :]
                else:
                    out_ref[group, chunk, place] = gated.astype(out_ref.dtype)
            total[chunk, :] = squares
        if first_layer:
            rows = length // cols
            for head in range(heads):
                for col in range(cols):
                    picked = staged[head, pl.ds(col, rows, stride=PITCH), :]
                    out_in[group, col, head * rows : (head + 1) * rows, :] = picked.astype(BF16)
            out_copy(group).start()
        return carry

    lax.fori_loop(0, groups, advance, 0)
    ordered = total[...]
    if first_layer:
        rows = length // cols
        ordered = jnp.concatenate([total[pl.ds(col, rows, stride=cols), :] for col in range(cols)], axis=0)
    ones = jnp.ones((TILE, LANES), BF16)
    sums = jnp.zeros((TILE, length), F32)
    for part in split_two(ordered):
        sums = sums + lax.dot_general(ones, part, (((1,), (1,)), ((), ())), preferred_element_type=F32)
    if first_layer:
        high, middle, low = [part.astype(F32) for part in split_three(sums)]
        row = lax.broadcasted_iota(jnp.int32, (TILE, length), 0)
        parts = jnp.where(row == 0, high, jnp.where(row == 1, middle, low))
        parts = jnp.where(row < 3, parts, 0.0)
        empty = jnp.zeros((EXTRA - TILE, LANES), F32)
        for col in range(cols):
            start = col * rows
            inside = start % LANES
            tile = parts[:, start - inside : start - inside + LANES]
            if inside:
                tile = pltpu.roll(tile, LANES - inside, 1)
            extra[col, :, :] = jnp.concatenate([tile, empty], axis=0).astype(BF16)
        last = out_hbm.at[:, pl.ds(out_hbm.shape[1] - EXTRA, EXTRA), :]
        extra_copy = pltpu.make_async_copy(extra, last, sent.at[groups])
        extra_copy.start()
        extra_copy.wait()
        for group in range(groups):
            out_copy(group).wait()
    else:
        squares_ref[...] = sums[:1]


def gated_outputs(first_layer, own, factor, prior, cols):
    groups, length, part = factor.shape
    heads = part // LANES
    width = groups * part
    scratch = [
        pltpu.VMEM((groups, length, part), own.dtype),
        pltpu.VMEM((groups, length, part), factor.dtype),
        pltpu.VMEM((length, LANES), own.dtype),
    ]
    total = pltpu.VMEM((length, LANES), F32)
    got = pltpu.SemaphoreType.DMA((2 * groups + 1,))
    if first_layer:
        rows = length // cols
        out_specs = HBM
        out_shape = jax.ShapeDtypeStruct((cols, width // LANES * rows + EXTRA, LANES), BF16)
        scratch += [
            pltpu.VMEM((groups, cols, heads * rows, LANES), BF16),
            total,
            pltpu.SemaphoreType.DMA((groups + 1,)),
            got,
            pltpu.VMEM((heads, rows * PITCH, LANES), F32),
            pltpu.VMEM((cols, EXTRA, LANES), BF16),
        ]
    else:
        out_specs = [VMEM, VMEM]
        out_shape = [
            jax.ShapeDtypeStruct((groups, length, part), LAST_TYPE),
            jax.ShapeDtypeStruct((1, length), F32),
        ]
        scratch += [total, got]
    return pl.pallas_call(
        functools.partial(gated_kernel, first_layer),
        in_specs=[HBM, HBM, VMEM],
        out_specs=out_specs,
        out_shape=out_shape,
        scratch_shapes=scratch,
        compiler_params=params(GATED_MB[first_layer]),
        cost_estimate=pl.CostEstimate(
            flops=1_200_000_000, bytes_accessed=13_000_000, transcendentals=2_000_000
        ),
        name="gated",
    )(own, factor, prior)


def scaled_kernel(features, gated_ref, gain_ref, *refs):
    *squares_refs, out_hbm, out_in, sent = refs
    parts, rows, width = out_in.shape
    part_lanes = gated_ref.shape[2]

    def out_copy(part):
        place = pl.ds(pl.multiple_of(part * rows, rows), rows)
        return pltpu.make_async_copy(out_in.at[part], out_hbm.at[place], sent.at[part])

    def advance(part, carry):
        at = pl.ds(pl.multiple_of(part * rows, rows), rows)
        scale = norm_scale(sum(ref[:, at] for ref in squares_refs), features)
        column = jnp.transpose(jnp.broadcast_to(scale, (LANES, rows)))
        for head in range(width // LANES):
            place = slice(head * LANES, (head + 1) * LANES)
            group, inside = divmod(head * LANES, part_lanes)
            gated = gated_ref[group, at, inside : inside + LANES].astype(F32) * column
            out_in[part, :, place] = (gated * gain_ref[:, place]).astype(BF16)
        out_copy(part).start()
        return carry

    lax.fori_loop(0, parts, advance, 0)
    for part in range(parts):
        out_copy(part).wait()


def scaled_outputs(gated, squares, gain, features):
    groups, length, part_lanes = gated.shape
    width = groups * part_lanes
    parts = length // SCALED_ROWS
    return pl.pallas_call(
        functools.partial(scaled_kernel, features),
        in_specs=[VMEM] * (2 + len(squares)),
        out_specs=HBM,
        out_shape=jax.ShapeDtypeStruct((length, width), BF16),
        scratch_shapes=[
            pltpu.VMEM((parts, SCALED_ROWS, width), BF16),
            pltpu.SemaphoreType.DMA((parts,)),
        ],
        compiler_params=params(48),
        name="scaled",
    )(gated, gain, *squares)


def over_head(value):
    devices = lax.axis_size("head")
    others = [
        lax.ppermute(value, "head", [(at, at ^ step) for at in range(devices)]) for step in range(1, devices)
    ]
    return [value, *others]


def body(
    tokens_in,
    gate_rows,
    gate_cols,
    write_rows,
    read_rows,
    step_rows,
    decay_rows,
    skip_rows,
    norm_rows,
    write_cols,
    read_cols,
    step_cols,
    decay_cols,
    skip_cols,
    norm_cols,
):
    grid_rows, grid_cols, width = tokens_in.shape
    devices = lax.axis_size(SEQ)
    features = float(width * lax.axis_size("head"))
    tokens = grid_rows * grid_cols
    column_len = gate_cols.shape[0]

    x = tokens_in.reshape(tokens, width)
    payload, before = device_states(x, write_rows, step_rows, decay_rows, None, None, features, devices)
    half = tokens // BLOCK // 2
    gate = gate_rows.reshape(tokens, width)
    local = lambda first, decay, done: local_factors(
        first, half, x, write_rows, read_rows, step_rows, decay, gate, None, None, before, skip_rows, features, done
    )
    prior, done, decay = prior_states(payload, local(0, decay_rows, ()), decay_rows)
    hidden = gated_outputs(True, *local(half, decay, done), prior, grid_cols)
    hidden = lax.all_to_all(hidden, SEQ, split_axis=0, concat_axis=0, tiled=True)
    squares = hidden[:, -EXTRA : 3 - EXTRA, :grid_rows].astype(F32)
    squares = (squares[:, 0] + squares[:, 1] + squares[:, 2]).reshape(-1, LANES)
    squares = [sum(over_head(squares))]

    gain = norm_rows[None]
    payload, before = device_states(
        hidden, write_cols, step_cols, decay_cols, squares, gain, features, devices
    )
    half = column_len // BLOCK // 2
    gate = gate_cols.reshape(column_len, width)
    local = lambda first, decay, done: local_factors(
        first, half, hidden, write_cols, read_cols, step_cols, decay, gate, squares, gain, before, skip_cols, features, done
    )
    prior, done, decay = prior_states(payload, local(0, decay_cols, ()), decay_cols)
    gated, last_squares = gated_outputs(False, *local(half, decay, done), prior, 1)
    last_squares = over_head(last_squares)
    out = scaled_outputs(gated, last_squares, norm_cols[None], features)
    return out.reshape(column_len, 1, width)


def solution(mesh):
    torus = Mesh(
        mesh.devices.reshape(4, 4, 2, mesh.shape["head"]), ("seq_0", "seq_1", "seq_2", "head")
    )
    return jax.shard_map(
        body,
        mesh=torus,
        in_specs=(
            P(SEQ, None, "head"),
            P(SEQ, None, "head"),
            P(None, SEQ, "head"),
            P(None, SEQ),
            P(None, SEQ),
            P("head", SEQ),
            P("head", SEQ),
            P("head"),
            P("head"),
            P(None, SEQ),
            P(None, SEQ),
            P("head", SEQ),
            P("head", SEQ),
            P("head"),
            P("head"),
        ),
        out_specs=P(None, SEQ, "head"),
        check_vma=False,
    )
```

```python
import functools

import jax
import jax.numpy as jnp
from jax import lax
from jax.experimental import pallas as pl
from jax.experimental.pallas import tpu as pltpu
from jax.sharding import Mesh
from jax.sharding import PartitionSpec as P

BLOCK = 256
SEQ = ("seq_0", "seq_1", "seq_2")
EPSILON = 1e-05
LANES = 128
TILE = 8
HEADS_PER_STEP = 3
EXTRA = 16
CHUNK = 128
PITCH = 40
STATES_MB = 53
LOG2E = 1.4426950408889634
OWN_TYPE = jnp.float32
FACTOR_TYPE = jnp.bfloat16
LAST_TYPE = jnp.bfloat16
SCALED_ROWS = 128
GATED_MB = (49, 52)
MEGABYTE = 1024 * 1024
F32 = jnp.float32
BF16 = jnp.bfloat16


def params(megabytes=56):
    return pltpu.CompilerParams(vmem_limit_bytes=megabytes * MEGABYTE)


def split_three(value):
    high = value.astype(BF16)
    rest = value - high.astype(F32)
    middle = rest.astype(BF16)
    low = (rest - middle.astype(F32)).astype(BF16)
    return high, middle, low


def split_two(value):
    high = value.astype(BF16)
    return high, (value - high.astype(F32)).astype(BF16)


def running_sums(decay):
    length = decay.shape[1]
    earlier = lax.broadcasted_iota(jnp.int32, (length, length), 0)
    later = lax.broadcasted_iota(jnp.int32, (length, length), 1)
    upper = jnp.where(earlier <= later, 1.0, 0.0).astype(BF16)
    high, middle, low = split_three(decay)
    total = jnp.dot(low, upper, preferred_element_type=F32)
    total = total + jnp.dot(middle, upper, preferred_element_type=F32)
    return total + jnp.dot(high, upper, preferred_element_type=F32)


def norm_scale(squares, features):
    return lax.rsqrt(squares / features + EPSILON)


def head_inputs(x_ref, head, by_head):
    if by_head:
        rows = BLOCK // x_ref.shape[0]
        return x_ref[:, head * rows : (head + 1) * rows, :].reshape(BLOCK, LANES)
    return x_ref[:, head * LANES : (head + 1) * LANES]


def block_scale(squares_refs, block, features):
    rows = BLOCK // LANES
    squares = sum(ref[pl.ds(block * rows, rows), :] for ref in squares_refs)
    pieces = [squares[row : row + 1, :] for row in range(rows)]
    return norm_scale(jnp.concatenate(pieces, axis=1), features)


HBM = pl.BlockSpec(memory_space=pltpu.HBM)
VMEM = pl.BlockSpec(memory_space=pltpu.VMEM)


def silu(value):
    return value * pl.reciprocal(1.0 + jnp.exp(-value), approx=True)


def states_kernel(by_head, features, x_ref, write_hbm, step_hbm, decay_hbm, *refs):
    if by_head:
        *squares_hbms, gain_hbm, payload_hbm, before_hbm, gain_ref, squares_ref, write_ref, step_ref, decay_ref, before, payload, total, sent, got = refs
    else:
        payload_hbm, before_hbm, x_in, write_ref, step_ref, decay_ref, before, payload, total, sent, got = refs
    head_count = step_ref.shape[0]
    state_size = write_ref.shape[0]
    blocks = before.shape[0] - 1
    pairs = ((decay_hbm, decay_ref), (step_hbm, step_ref), (write_hbm, write_ref))
    if by_head:
        squares_refs = [squares_ref.at[at] for at in range(len(squares_hbms))]
        pairs += ((gain_hbm, gain_ref), *zip(squares_hbms, squares_refs))
    small = [pltpu.make_async_copy(*pair, got.at[at]) for at, pair in enumerate(pairs)]

    def x_copy(block):
        rows = x_in.shape[1]
        place = pl.ds(pl.multiple_of(block * rows, rows), rows)
        return pltpu.make_async_copy(x_ref.at[place], x_in.at[block], got.at[len(pairs) + block])

    def before_copy(block):
        return pltpu.make_async_copy(before.at[block], before_hbm.at[block], sent.at[block])

    for copy in small:
        copy.start()
    if not by_head:
        for block in range(blocks):
            x_copy(block).start()
    before[0] = jnp.zeros(before.shape[1:], F32)
    total[...] = jnp.zeros_like(total)
    for copy in small:
        copy.wait()

    def advance(block, carry):
        positions = pl.ds(pl.multiple_of(block * BLOCK, BLOCK), BLOCK)
        before_copy(block).start()
        cumulative = running_sums(decay_ref[:, positions])
        final = cumulative[:, BLOCK - 1 :]
        weights = jnp.exp(final - cumulative) * step_ref[:, positions]
        if by_head:
            weights = weights * block_scale(squares_refs, block, features)
        if by_head:
            devices = x_ref.shape[0] // blocks
            x_block = x_ref.at[pl.ds(pl.multiple_of(block * devices, devices), devices)]
        else:
            x_copy(block).wait()
            x_block = x_in.at[block]
        fading = jnp.broadcast_to(jnp.exp(final), (head_count, LANES))
        write = write_ref[:, positions].astype(F32)
        for head in range(head_count):
            loaded = (write * weights[head : head + 1, :]).astype(BF16)
            gained = jnp.dot(loaded, head_inputs(x_block, head, by_head), preferred_element_type=F32)
            if by_head:
                gained = gained * gain_ref[:, head * LANES : (head + 1) * LANES]
            rows = slice(head * state_size, (head + 1) * state_size)
            before[block + 1, rows, :] = fading[head : head + 1, :] * before[block, rows, :] + gained
        total[...] = total[...] + jnp.broadcast_to(final, (head_count, LANES))
        return carry

    lax.fori_loop(0, blocks, advance, 0)
    devices, height = payload.shape[0], payload.shape[1] - TILE
    payload[:, :height, :] = before[blocks].reshape(devices, height, LANES)
    for device in range(devices):
        for tile in range(height // TILE):
            head = (device * height + tile * TILE) // state_size
            payload[device, height + tile : height + tile + 1, :] = total[head : head + 1, :]
        left = height + height // TILE
        payload[device, left:, :] = jnp.zeros((height + TILE - left, LANES), F32)
    out = pltpu.make_async_copy(payload, payload_hbm, sent.at[blocks])
    out.start()
    for block in range(blocks):
        before_copy(block).wait()
    out.wait()


def device_states(x, write, step, decay, squares, gain, features, devices):
    head_count, length = step.shape
    state_size = write.shape[0]
    blocks = length // BLOCK
    height = head_count * state_size // devices
    by_head = squares is not None
    specs = [VMEM if by_head else HBM] + [HBM] * 3
    operands = [x, write, step, decay]
    scratch = []
    if by_head:
        specs += [HBM] * (len(squares) + 1)
        operands += [*squares, gain]
        scratch += [pltpu.VMEM(gain.shape, F32), pltpu.VMEM((len(squares), *squares[0].shape), F32)]
    else:
        scratch.append(pltpu.VMEM((blocks, x.shape[0] // blocks, *x.shape[1:]), BF16))
    return pl.pallas_call(
        functools.partial(states_kernel, by_head, features),
        in_specs=specs,
        out_specs=[HBM, HBM],
        out_shape=[
            jax.ShapeDtypeStruct((devices, height + TILE, LANES), F32),
            jax.ShapeDtypeStruct((blocks, head_count * state_size, LANES), F32),
        ],
        scratch_shapes=scratch
        + [
            pltpu.VMEM(write.shape, BF16),
            pltpu.VMEM(step.shape, F32),
            pltpu.VMEM(decay.shape, F32),
            pltpu.VMEM((blocks + 1, head_count * state_size, LANES), F32),
            pltpu.VMEM((devices, height + TILE, LANES), F32),
            pltpu.VMEM((head_count, LANES), F32),
            pltpu.SemaphoreType.DMA((blocks + 1,)),
            pltpu.SemaphoreType.DMA((len(operands) + blocks,)),
        ],
        compiler_params=params(STATES_MB if by_head else 56),
        cost_estimate=pl.CostEstimate(flops=500_000_000, bytes_accessed=6_000_000, transcendentals=20_000),
        name="states",
    )(*operands)


def prefix_kernel(ends_ref, prior_ref):
    devices, height, _ = prior_ref.shape
    running = [jnp.zeros((TILE, LANES), F32) for _ in range(height // TILE)]
    for device in range(devices):
        for tile in range(height // TILE):
            rows = slice(tile * TILE, (tile + 1) * TILE)
            prior_ref[device, rows, :] = running[tile]
            fade = jnp.exp(ends_ref[device, height + tile : height + tile + 1, :])
            running[tile] = fade * running[tile] + ends_ref[device, rows, :]


def prior_states(payload, beside, later):
    devices, height, _ = payload.shape
    height = height - TILE
    ends = lax.all_to_all(payload, SEQ, split_axis=0, concat_axis=0, tiled=True)
    ends, beside, later = lax.optimization_barrier((ends, beside, later))
    prior = pl.pallas_call(
        prefix_kernel,
        out_shape=jax.ShapeDtypeStruct((devices, height, LANES), F32),
        compiler_params=params(8),
        name="prefix",
    )(ends)
    prior = lax.all_to_all(prior, SEQ, split_axis=0, concat_axis=0, tiled=True)
    return prior.reshape(devices * height, LANES), beside, later


def read_state(reads, state):
    parts = jnp.concatenate(split_two(state), axis=0)
    return jnp.dot(reads, parts, preferred_element_type=F32)


def local_kernel(by_head, features, first, parts, *refs):
    x_ref, write_ref, read_ref, step_ref, decay_ref, gate_ref, before_ref, skip_ref = refs[:8]
    if by_head:
        *squares_refs, gain_ref = refs[8 : 9 + parts]
    own_ref, factor_ref, total = refs[-3:]
    head_count = step_ref.shape[0]
    state_size = write_ref.shape[0]
    half = BLOCK // 2
    block = first + pl.program_id(0)

    @pl.when(pl.program_id(0) == 0)
    def _():
        total[...] = jnp.zeros_like(total)
        if first:
            earlier = jnp.sum(decay_ref[:, : first * BLOCK], axis=1, keepdims=True)
            total[...] = jnp.broadcast_to(earlier, total.shape)

    cumulative = running_sums(decay_ref[:, pl.ds(pl.multiple_of(block * BLOCK, BLOCK), BLOCK)])
    step = step_ref[...]
    if by_head:
        scale = block_scale(squares_refs, block, features)
        step = step * scale
        scale_column = jnp.transpose(jnp.broadcast_to(scale, (LANES, BLOCK)))
    padding = jnp.zeros((LANES - head_count, BLOCK), F32)
    columns = jnp.transpose(jnp.concatenate([cumulative, padding], axis=0))
    lifts = jnp.exp(columns)
    columns = columns * LOG2E
    lowered = (cumulative - jnp.log(step)) * LOG2E
    kept = jnp.exp(total[...])
    total[...] = total[...] + jnp.broadcast_to(cumulative[:, BLOCK - 1 :], (head_count, LANES))
    read = read_ref[...]
    turned = jnp.transpose(read.astype(F32))
    reads = jnp.concatenate([turned, turned], axis=1)
    own_ref[own_ref.shape[0] - 1] = jnp.concatenate([reads] * HEADS_PER_STEP, axis=1).astype(own_ref.dtype)
    reads = reads.astype(BF16)
    scores = lax.dot_general(read, write_ref[...], (((0,), (0,)), ((), ())), preferred_element_type=F32)
    first_half, last_half = slice(0, half), slice(half, BLOCK)
    causal = lax.broadcasted_iota(jnp.int32, (half, half), 0) >= lax.broadcasted_iota(
        jnp.int32, (half, half), 1
    )
    for head in range(head_count):
        row = lowered[head : head + 1, :]
        column = jnp.broadcast_to(columns[:, head : head + 1], (BLOCK, LANES))

        def mixing(t, s):
            spread = column[t] - row[:, s]
            if t == s:
                spread = jnp.where(causal, spread, -jnp.inf)
            return (jnp.exp2(spread) * scores[t, s]).astype(BF16)

        x = head_inputs(x_ref, head, by_head)
        upper = jnp.dot(mixing(first_half, first_half), x[first_half], preferred_element_type=F32)
        both = jnp.concatenate([mixing(last_half, first_half), mixing(last_half, last_half)], axis=1)
        lower = jnp.dot(both, x, preferred_element_type=F32)
        state = before_ref[0, head * state_size : (head + 1) * state_size, :]
        place = slice(head * LANES, (head + 1) * LANES)
        skipped = skip_ref[head] * x.astype(F32)
        outputs = jnp.concatenate([upper, lower], axis=0)
        if by_head:
            outputs = (outputs + skipped * scale_column) * gain_ref[:, place]
        else:
            outputs = outputs + skipped
        lift = jnp.broadcast_to(lifts[:, head : head + 1], (BLOCK, LANES))
        outputs = outputs + lift * read_state(reads, state)
        gate = silu(gate_ref[:, place].astype(F32))
        group, inside = divmod(head, HEADS_PER_STEP)
        inside = slice(inside * LANES, (inside + 1) * LANES)
        own_ref[group, :, inside] = (outputs * gate).astype(own_ref.dtype)
        factor_ref[group, :, inside] = (lift * kept[head : head + 1, :] * gate).astype(factor_ref.dtype)


def local_factors(first, count, x, write, read, step, decay, gate, squares, gain, before, skip, features, done):
    head_count, length = step.shape
    state_size = write.shape[0]
    blocks = length // BLOCK
    width = head_count * LANES
    by_head = squares is not None
    if by_head:
        x_spec = pl.BlockSpec((x.shape[0] // blocks, *x.shape[1:]), lambda k: (first + k, 0, 0))
    else:
        x_spec = pl.BlockSpec((BLOCK, width), lambda k: (first + k, 0))
    along = lambda rows: pl.BlockSpec((rows, BLOCK), lambda k: (0, first + k))
    specs = [
        x_spec,
        along(state_size),
        along(state_size),
        along(head_count),
        pl.BlockSpec((head_count, length), lambda k: (0, 0)),
        pl.BlockSpec((BLOCK, width), lambda k: (first + k, 0)),
        pl.BlockSpec((1, head_count * state_size, LANES), lambda k: (first + k, 0, 0)),
        pl.BlockSpec(memory_space=pltpu.SMEM),
    ]
    operands = [x, write, read, step, decay, gate, before, skip]
    if by_head:
        specs += [pl.BlockSpec(part.shape, lambda k: (0, 0)) for part in squares]
        specs.append(pl.BlockSpec((1, width), lambda k: (0, 0)))
        operands += [*squares, gain]
    part = HEADS_PER_STEP * LANES
    groups = width // part
    aliases = {len(operands) + at: at for at in range(len(done))}
    return pl.pallas_call(
        functools.partial(local_kernel, by_head, features, first, len(squares) if by_head else 0),
        grid=(count,),
        in_specs=specs + [HBM] * len(done),
        input_output_aliases=aliases,
        out_specs=[
            pl.BlockSpec((groups + 1, BLOCK, part), lambda k: (0, first + k, 0)),
            pl.BlockSpec((groups, BLOCK, part), lambda k: (0, first + k, 0)),
        ],
        out_shape=[
            jax.ShapeDtypeStruct((groups + 1, length, part), OWN_TYPE),
            jax.ShapeDtypeStruct((groups, length, part), FACTOR_TYPE),
        ],
        scratch_shapes=[pltpu.VMEM((head_count, LANES), F32)],
        compiler_params=params(),
        cost_estimate=pl.CostEstimate(
            flops=3_000_000_000, bytes_accessed=10_000_000, transcendentals=3_000_000
        ),
        name="local",
    )(*operands, *done)


def gated_kernel(first_layer, own_hbm, factor_hbm, prior_ref, *refs):
    if first_layer:
        out_hbm, own, factor, side, out_in, total, sent, got, staged, extra = refs
        cols = out_hbm.shape[0]
    else:
        out_ref, squares_ref, own, factor, side, total, got = refs
    groups, length, width = own.shape
    heads = width // LANES
    state_size = LANES // 2

    def in_copies(group):
        own_copy = pltpu.make_async_copy(own_hbm.at[group], own.at[group], got.at[group])
        at = groups + group
        return own_copy, pltpu.make_async_copy(factor_hbm.at[group], factor.at[group], got.at[at])

    side_copy = pltpu.make_async_copy(own_hbm.at[groups, :, pl.ds(0, LANES)], side, got.at[2 * groups])

    def out_copy(group):
        rows = out_in.shape[2]
        place = out_hbm.at[:, pl.ds(pl.multiple_of(group * rows, rows), rows), :]
        return pltpu.make_async_copy(out_in.at[group], place, sent.at[group])

    side_copy.start()
    for group in range(groups):
        for copy in in_copies(group):
            copy.start()
    total[...] = jnp.zeros_like(total)
    side_copy.wait()

    def advance(group, carry):
        depth = heads * state_size
        state = prior_ref[pl.ds(pl.multiple_of(group * depth, depth), depth), :]
        states = [state[head * state_size : (head + 1) * state_size, :] for head in range(heads)]
        parts = jnp.concatenate(split_two(jnp.concatenate(states, axis=1)), axis=0)
        for copy in in_copies(group):
            copy.wait()
        for start in range(0, length, CHUNK):
            chunk = slice(start, start + CHUNK)
            from_state = jnp.dot(side[chunk, :].astype(BF16), parts, preferred_element_type=F32)
            squares = total[chunk, :]
            for head in range(heads):
                place = slice(head * LANES, (head + 1) * LANES)
                gated = own[group, chunk, place].astype(F32)
                gated = gated + factor[group, chunk, place].astype(F32) * from_state[:, place]
                squares = squares + gated * gated
                if first_layer:
                    for row in range(CHUNK // cols):
                        pitched = pl.ds((start // cols + row) * PITCH, cols)
                        staged[head, pitched, :] = gated[row * cols : (row + 1) * cols, :]
                else:
                    out_ref[group, chunk, place] = gated.astype(out_ref.dtype)
            total[chunk, :] = squares
        if first_layer:
            rows = length // cols
            for head in range(heads):
                for col in range(cols):
                    picked = staged[head, pl.ds(col, rows, stride=PITCH), :]
                    out_in[group, col, head * rows : (head + 1) * rows, :] = picked.astype(BF16)
            out_copy(group).start()
        return carry

    lax.fori_loop(0, groups, advance, 0)
    ordered = total[...]
    if first_layer:
        rows = length // cols
        ordered = jnp.concatenate([total[pl.ds(col, rows, stride=cols), :] for col in range(cols)], axis=0)
    ones = jnp.ones((TILE, LANES), BF16)
    sums = jnp.zeros((TILE, length), F32)
    for part in split_two(ordered):
        sums = sums + lax.dot_general(ones, part, (((1,), (1,)), ((), ())), preferred_element_type=F32)
    if first_layer:
        high, middle, low = [part.astype(F32) for part in split_three(sums)]
        row = lax.broadcasted_iota(jnp.int32, (TILE, length), 0)
        parts = jnp.where(row == 0, high, jnp.where(row == 1, middle, low))
        parts = jnp.where(row < 3, parts, 0.0)
        empty = jnp.zeros((EXTRA - TILE, LANES), F32)
        for col in range(cols):
            start = col * rows
            inside = start % LANES
            tile = parts[:, start - inside : start - inside + LANES]
            if inside:
                tile = pltpu.roll(tile, LANES - inside, 1)
            extra[col, :, :] = jnp.concatenate([tile, empty], axis=0).astype(BF16)
        last = out_hbm.at[:, pl.ds(out_hbm.shape[1] - EXTRA, EXTRA), :]
        extra_copy = pltpu.make_async_copy(extra, last, sent.at[groups])
        extra_copy.start()
        extra_copy.wait()
        for group in range(groups):
            out_copy(group).wait()
    else:
        squares_ref[...] = sums[:1]


def gated_outputs(first_layer, own, factor, prior, cols):
    groups, length, part = factor.shape
    heads = part // LANES
    width = groups * part
    scratch = [
        pltpu.VMEM((groups, length, part), own.dtype),
        pltpu.VMEM((groups, length, part), factor.dtype),
        pltpu.VMEM((length, LANES), own.dtype),
    ]
    total = pltpu.VMEM((length, LANES), F32)
    got = pltpu.SemaphoreType.DMA((2 * groups + 1,))
    if first_layer:
        rows = length // cols
        out_specs = HBM
        out_shape = jax.ShapeDtypeStruct((cols, width // LANES * rows + EXTRA, LANES), BF16)
        scratch += [
            pltpu.VMEM((groups, cols, heads * rows, LANES), BF16),
            total,
            pltpu.SemaphoreType.DMA((groups + 1,)),
            got,
            pltpu.VMEM((heads, rows * PITCH, LANES), F32),
            pltpu.VMEM((cols, EXTRA, LANES), BF16),
        ]
    else:
        out_specs = [VMEM, VMEM]
        out_shape = [
            jax.ShapeDtypeStruct((groups, length, part), LAST_TYPE),
            jax.ShapeDtypeStruct((1, length), F32),
        ]
        scratch += [total, got]
    return pl.pallas_call(
        functools.partial(gated_kernel, first_layer),
        in_specs=[HBM, HBM, VMEM],
        out_specs=out_specs,
        out_shape=out_shape,
        scratch_shapes=scratch,
        compiler_params=params(GATED_MB[first_layer]),
        cost_estimate=pl.CostEstimate(
            flops=1_200_000_000, bytes_accessed=13_000_000, transcendentals=2_000_000
        ),
        name="gated",
    )(own, factor, prior)


def scaled_kernel(features, gated_ref, gain_ref, *refs):
    *squares_refs, out_hbm, out_in, sent = refs
    parts, rows, width = out_in.shape
    part_lanes = gated_ref.shape[2]

    def out_copy(part):
        place = pl.ds(pl.multiple_of(part * rows, rows), rows)
        return pltpu.make_async_copy(out_in.at[part], out_hbm.at[place], sent.at[part])

    def advance(part, carry):
        at = pl.ds(pl.multiple_of(part * rows, rows), rows)
        scale = norm_scale(sum(ref[:, at] for ref in squares_refs), features)
        column = jnp.transpose(jnp.broadcast_to(scale, (LANES, rows)))
        for head in range(width // LANES):
            place = slice(head * LANES, (head + 1) * LANES)
            group, inside = divmod(head * LANES, part_lanes)
            gated = gated_ref[group, at, inside : inside + LANES].astype(F32) * column
            out_in[part, :, place] = (gated * gain_ref[:, place]).astype(BF16)
        out_copy(part).start()
        return carry

    lax.fori_loop(0, parts, advance, 0)
    for part in range(parts):
        out_copy(part).wait()


def scaled_outputs(gated, squares, gain, features):
    groups, length, part_lanes = gated.shape
    width = groups * part_lanes
    parts = length // SCALED_ROWS
    return pl.pallas_call(
        functools.partial(scaled_kernel, features),
        in_specs=[VMEM] * (2 + len(squares)),
        out_specs=HBM,
        out_shape=jax.ShapeDtypeStruct((length, width), BF16),
        scratch_shapes=[
            pltpu.VMEM((parts, SCALED_ROWS, width), BF16),
            pltpu.SemaphoreType.DMA((parts,)),
        ],
        compiler_params=params(48),
        name="scaled",
    )(gated, gain, *squares)


def over_head(value):
    devices = lax.axis_size("head")
    others = [
        lax.ppermute(value, "head", [(at, at ^ step) for at in range(devices)]) for step in range(1, devices)
    ]
    return [value, *others]


def body(
    tokens_in,
    gate_rows,
    gate_cols,
    write_rows,
    read_rows,
    step_rows,
    decay_rows,
    skip_rows,
    norm_rows,
    write_cols,
    read_cols,
    step_cols,
    decay_cols,
    skip_cols,
    norm_cols,
):
    grid_rows, grid_cols, width = tokens_in.shape
    devices = lax.axis_size(SEQ)
    features = float(width * lax.axis_size("head"))
    tokens = grid_rows * grid_cols
    column_len = gate_cols.shape[0]

    x = tokens_in.reshape(tokens, width)
    payload, before = device_states(x, write_rows, step_rows, decay_rows, None, None, features, devices)
    half = tokens // BLOCK // 2
    gate = gate_rows.reshape(tokens, width)
    local = lambda first, decay, done: local_factors(
        first, half, x, write_rows, read_rows, step_rows, decay, gate, None, None, before, skip_rows, features, done
    )
    prior, done, decay = prior_states(payload, local(0, decay_rows, ()), decay_rows)
    hidden = gated_outputs(True, *local(half, decay, done), prior, grid_cols)
    hidden = lax.all_to_all(hidden, SEQ, split_axis=0, concat_axis=0, tiled=True)
    squares = hidden[:, -EXTRA : 3 - EXTRA, :grid_rows].astype(F32)
    squares = (squares[:, 0] + squares[:, 1] + squares[:, 2]).reshape(-1, LANES)
    squares = [sum(over_head(squares))]

    gain = norm_rows[None]
    payload, before = device_states(
        hidden, write_cols, step_cols, decay_cols, squares, gain, features, devices
    )
    half = column_len // BLOCK // 2
    gate = gate_cols.reshape(column_len, width)
    local = lambda first, decay, done: local_factors(
        first, half, hidden, write_cols, read_cols, step_cols, decay, gate, squares, gain, before, skip_cols, features, done
    )
    prior, done, decay = prior_states(payload, local(0, decay_cols, ()), decay_cols)
    gated, last_squares = gated_outputs(False, *local(half, decay, done), prior, 1)
    last_squares = over_head(last_squares)
    out = scaled_outputs(gated, last_squares, norm_cols[None], features)
    return out.reshape(column_len, 1, width)


def solution(mesh):
    torus = Mesh(
        mesh.devices.reshape(4, 4, 2, mesh.shape["head"]), ("seq_0", "seq_1", "seq_2", "head")
    )
    return jax.shard_map(
        body,
        mesh=torus,
        in_specs=(
            P(SEQ, None, "head"),
            P(SEQ, None, "head"),
            P(None, SEQ, "head"),
            P(None, SEQ),
            P(None, SEQ),
            P("head", SEQ),
            P("head", SEQ),
            P("head"),
            P("head"),
            P(None, SEQ),
            P(None, SEQ),
            P("head", SEQ),
            P("head", SEQ),
            P("head"),
            P("head"),
        ),
        out_specs=P(None, SEQ, "head"),
        check_vma=False,
    )
```
